256 devices in a mesh: row: 16 (over x_lo, y, core), col: 16 (over z, x_hi).
Axes of the slice: x: 4 (x_hi: 2, x_lo: 2; x = x_hi * 2 + x_lo), y: 4, z: 8, core: 2. Of those that a mesh axis runs over, the one named last changes fastest.
Arguments:
- images: bfloat16 [1152, 16384], P('col', 'row')
- texts: bfloat16 [1152, 16384], P('row', 'col')
- pairs: int32 [16384], P('row'), may hold values from 0 to 16383, as said below
- log_scale: float32 [1], replicated, may hold values from 2 to 2.6
- bias: float32 [1], replicated, may hold values from -8 to -6
Outputs:
- row_loss: float32 [16384], P('row')
- image_grad: float32 [1152, 16384], P('col', 'row')
- text_grad: float32 [1152, 16384], P('row', 'col')
The draws below stay inside these ranges and needn't reach their ends.
Inputs may be any that keep to these rules, and one draw needn't show every extreme that they name: pairs is a permutation of the 16384 caption indices.
All inputs are finite; a program needn't handle non-finite values.
Results may differ from the reference program's by a relative error of at most 0.0095.
Values may be sent and summed in bfloat16 or wider, within the bound.
No kernel may reach another device: no remote copies, remote signals or barrier semaphores. Data moves between devices by JAX's collectives and lax.ppermute only.
A program may use at most 64 MiB of HBM per device.

```python
import math
import jax
import jax.numpy as jnp
from jax import lax

D = 1152
ROWB = 1024
BATCH = 16384


centre_count = 64


feature_norm = 4.64


def shared_pairs(key):
    return jax.random.permutation(jax.random.fold_in(key, 11), BATCH).astype(jnp.int32)


def shared_directions(key, weight):
    centres = jax.random.normal(jax.random.fold_in(key, 21), (D, centre_count), jnp.float32)
    member = jax.random.randint(jax.random.fold_in(key, 22), (BATCH,), 0, centre_count)
    picked = centres[:, member]
    own = jax.random.normal(jax.random.fold_in(key, 23), (D, BATCH), jnp.float32)
    feature = jnp.exp(jax.random.uniform(jax.random.fold_in(key, 24), (D, 1), jnp.float32, 0.0, math.log(10.0))) / feature_norm
    direction = feature * (math.sqrt(weight) * picked + math.sqrt(1.0 - weight) * own)
    return (direction, feature)


def column_scales(key, lower, upper):
    return jnp.exp(jax.random.uniform(key, (1, BATCH), jnp.float32, math.log(lower), math.log(upper)))


def draw_images(key, part):
    weight = 0.5
    lower = 0.4
    upper = 4.0
    direction, feature = shared_directions(key, weight)
    key = jax.random.fold_in(key, 1)
    scales = column_scales(key, lower, upper)
    return (direction * scales / math.sqrt(D)).astype(jnp.bfloat16)


def draw_texts(key, part):
    weight = 0.5
    keep = 0.75
    lower = 0.4
    upper = 4.0
    direction, feature = shared_directions(key, weight)
    pairs = shared_pairs(key)
    key = jax.random.fold_in(key, 2)
    noise_key, scale_key = jax.random.split(key)
    noise = feature * jax.random.normal(noise_key, (D, BATCH), jnp.float32)
    mixed = keep * direction + math.sqrt(1.0 - keep * keep) * noise
    placed = jnp.zeros((D, BATCH), jnp.float32).at[:, pairs].set(mixed)
    scales = column_scales(scale_key, lower, upper)
    return (placed * scales / math.sqrt(D)).astype(jnp.bfloat16)


def draw_pairs(key, part):
    return shared_pairs(key)


def setup_inputs(seed: int = 0) -> dict:
    key_of = jax.random.split(jax.random.key(seed), 6)
    return {
        "images": draw_images(jax.random.fold_in(key_of[5], 71), 0),
        "texts": draw_texts(jax.random.fold_in(key_of[5], 71), 0),
        "pairs": draw_pairs(jax.random.fold_in(key_of[5], 71), 0),
        "log_scale": jnp.clip(jax.random.uniform(key_of[3], (1,), jnp.float32, 2.0, 2.6), 2.0, 2.6),
        "bias": jnp.clip(jax.random.uniform(key_of[4], (1,), jnp.float32, -8.0, -6.0), -8.0, -6.0),
    }


EPS = 1e-06

def unit_rows(values):
    wide = values.astype(jnp.float32)
    norm = jnp.sqrt(lax.optimization_barrier(jnp.sum(wide * wide, axis=1)) + EPS)
    return ((wide / norm[:, None]).astype(jnp.bfloat16), norm)

def project_rows(pull, unit, norm):
    unit_wide = unit.astype(jnp.float32)
    inner = lax.optimization_barrier(jnp.sum(unit_wide * pull, axis=1))
    return (pull - unit_wide * inner[:, None]) / norm[:, None]

def reference(images, texts, pairs, log_scale, bias):
    scale = jnp.exp(log_scale[0])
    shift = bias[0]
    image_unit, image_norm = unit_rows(images.T)
    text_unit, text_norm = unit_rows(texts.T)
    blocks = BATCH // ROWB
    unit_blocks = image_unit.reshape(blocks, ROWB, D)
    pair_blocks = pairs.reshape(blocks, ROWB)
    columns = jnp.arange(BATCH, dtype=jnp.int32)

    def step(text_acc, item):
        block_unit, block_pairs = item
        logits = jnp.dot(block_unit, text_unit.T, preferred_element_type=jnp.float32) * scale + shift
        sign = jnp.where(block_pairs[:, None] == columns[None, :], 1.0, -1.0).astype(jnp.float32)
        loss = lax.optimization_barrier(jnp.sum(jax.nn.softplus(-sign * logits), axis=1))
        coeff = (-sign * jax.nn.sigmoid(-sign * logits) * scale).astype(jnp.bfloat16)
        pull = jnp.dot(coeff, text_unit, preferred_element_type=jnp.float32)
        text_acc = text_acc + jnp.dot(coeff.T, block_unit, preferred_element_type=jnp.float32)
        return (text_acc, (loss, pull))
    start = jnp.zeros((BATCH, D), jnp.float32)
    text_pull, (loss, image_pull) = lax.scan(step, start, (unit_blocks, pair_blocks))
    row_loss = loss.reshape(BATCH)
    image_pull = image_pull.reshape(BATCH, D)
    image_grad = project_rows(image_pull, image_unit, image_norm)
    text_grad = project_rows(text_pull, text_unit, text_norm)
    return (row_loss, image_grad.T, text_grad.T)
```

```python
import functools

import jax
import jax.numpy as jnp
from jax import lax
from jax.experimental import pallas as pl
from jax.experimental.pallas import tpu as pltpu
from jax.sharding import PartitionSpec as P

EPS = 1e-06
F32 = jnp.float32
BF16 = jnp.bfloat16
NZ, NY = 8, 4
SH = 72
PAD = 80
N = 1024
HALF = N // 2
ROWS = 16 * PAD
VMEM_LIMIT = 56 * 1024 * 1024


def row_pairs(f):
    out = []
    for r in range(16):
        xlo, y, core = r // 8, (r // 2) % 4, r % 2
        a, b, c = f(xlo, y, core)
        out.append((r, (a * 4 + b) * 2 + c))
    return out


def col_pairs(f):
    out = []
    for r in range(16):
        a, b = f(r // 2, r % 2)
        out.append((r, a * 2 + b))
    return out


def shift_z(v, d):
    return lax.ppermute(v, "col", col_pairs(lambda z, h: ((z + d) % NZ, h)))


def shift_y(v, d):
    return lax.ppermute(v, "row", row_pairs(lambda x, y, c: (x, (y + d) % NY, c)))


def swap_xhi(v):
    return lax.ppermute(v, "col", col_pairs(lambda z, h: (z, 1 - h)))


def swap_xlo(v):
    return lax.ppermute(v, "row", row_pairs(lambda x, y, c: (1 - x, y, c)))


def swap_core(v):
    return lax.ppermute(v, "row", row_pairs(lambda x, y, c: (x, y, 1 - c)))


def xor_z(v, b):
    return lax.ppermute(v, "col", col_pairs(lambda z, h: (z ^ b, h)))


def ring_gather(v, shift, n):
    half = n // 2
    up = down = v
    out = {0: [v]}
    for k in range(1, half):
        up, down = shift(up, 1), shift(down, -1)
        out[n - k] = [up]
        out[k] = [down]
    out[half] = [shift(up[:, :HALF], 1), shift(down[:, HALF:], -1)]
    return out


def place_piece(ref, offset, pieces):
    if len(pieces) == 1:
        ref[pl.ds(offset, SH), :] = pieces[0][...]
    else:
        ref[pl.ds(offset, SH), :HALF] = pieces[0][...]
        ref[pl.ds(offset, SH), HALF:] = pieces[1][...]


def coords():
    row, col = lax.axis_index("row"), lax.axis_index("col")
    return row // 8, (row // 2) % 4, row % 2, col // 2, col % 2


def text_kernel(*refs):
    pieces, (yp, ypt, brow, bcol) = refs[:20], refs[20:]
    xlo, y, core, z, xhi = coords()
    yp[...] = jnp.zeros_like(yp)
    at = 0
    for swapped in range(2):
        for other in range(2):
            for k in range(NY):
                count = 2 if k == NY // 2 else 1
                group = pieces[at : at + count]
                at += count
                g = (xlo + other) % 2 * 4 + (y + k) % 4
                block = (g - z + NZ) % NZ * 2 + (core + swapped + xhi) % 2
                place_piece(yp, pl.multiple_of(block * PAD, 16), group)
    total = jnp.zeros((1, N), F32)
    for b in range(16):
        v = yp[b * PAD : (b + 1) * PAD, :].astype(F32)
        total += jnp.sum(v * v, axis=0, keepdims=True)
    brow[...] = lax.rsqrt(total + EPS)
    for c in range(N // 128):
        v = yp[:, c * 128 : (c + 1) * 128].T
        ypt[c * 128 : (c + 1) * 128, :] = v
        w = v.astype(F32)
        s = jnp.sum(w * w, axis=1, keepdims=True)
        bcol[c * 128 : (c + 1) * 128, :] = jnp.broadcast_to(lax.rsqrt(s + EPS), (128, 128))


def image_kernel(*refs):
    pieces = refs[:18]
    pairs, logscale, bias, yp, ypt, bcol = refs[18:24]
    xp, cx, sj, loss = refs[24:28]
    outs = refs[28:46]
    t_ref, cy, acc_loss, acc_si, acc_sj = refs[46:]
    at = 0
    xp[...] = jnp.zeros_like(xp)
    for other in range(2):
        for k in range(NZ):
            count = 2 if k == NZ // 2 else 1
            place_piece(xp, (2 * k + other) * PAD, pieces[at : at + count])
            at += count
    total = jnp.zeros((1, N), F32)
    for b in range(16):
        v = xp[b * PAD : (b + 1) * PAD, :].astype(F32)
        total += jnp.sum(v * v, axis=0, keepdims=True)
    a = lax.rsqrt(total + EPS)
    scale = jnp.exp(jnp.full((1, N), logscale[0], F32))
    ascale = a * scale
    shift = bias[0]
    scale_t = scale[:, :128]
    acc_loss[...] = jnp.zeros_like(acc_loss)
    acc_si[...] = jnp.zeros_like(acc_si)
    acc_sj[...] = jnp.zeros_like(acc_sj)
    first = lax.axis_index("col") * N
    W = 256
    for n in range(N // W):
        t_ref[:, n * W : (n + 1) * W] = jnp.dot(
            ypt[...], xp[:, n * W : (n + 1) * W], preferred_element_type=F32
        )
    for n in range(N // 128):
        cols = slice(n * 128, (n + 1) * 128)
        ai = a[:, cols]
        asc = ascale[:, cols]
        pair = pairs[:, cols]

        def body(j, carry, cols=cols, ai=ai, asc=asc, pair=pair):
            al, asi = carry
            rows = pl.ds(pl.multiple_of(j * 64, 64), 64)
            b = bcol[rows, :]
            t = t_ref[rows, cols] * b
            cos = t * ai
            logit = t * asc + shift
            ids = lax.broadcasted_iota(jnp.int32, (64, 128), 0) + (first + j * 64)
            hit = ids == pair
            e = jnp.exp(logit)
            sig = e / (1.0 + e)
            d = jnp.where(hit, sig - 1.0, sig) * scale_t
            dc = d * cos
            cy[rows, cols] = (d * b).astype(BF16)
            cx[rows, cols] = (d * ai).astype(BF16)
            acc_sj[rows, :] += dc
            e8 = e.reshape(8, 8, 128)
            q = e8[0]
            for m in range(1, 8):
                q = q + e8[m] + q * e8[m]
            soft = jnp.where(q < 1e-4, (1.0 - 0.5 * q) * q, jnp.log(1.0 + q))
            al = al + soft - jnp.sum(jnp.where(hit, logit, 0.0).reshape(8, 8, 128), axis=0)
            asi = asi + jnp.sum(dc.reshape(8, 8, 128), axis=0)
            return al, asi

        zero = jnp.zeros((8, 128), F32)
        al, asi = lax.fori_loop(0, N // 64, body, (zero, zero))
        acc_loss[:, cols] = al
        acc_si[:, cols] = asi
    loss[...] = jnp.sum(acc_loss[...], axis=0, keepdims=True)
    si = jnp.sum(acc_si[...], axis=0, keepdims=True)
    sj[...] = jnp.sum(acc_sj[...].T, axis=0, keepdims=True)
    for n in range(N // W):
        cols = slice(n * W, (n + 1) * W)
        pull = jnp.dot(yp[...], cy[:, cols], preferred_element_type=F32)
        ai, sn = a[:, cols], si[:, cols]
        at = 0
        for other in range(2):
            for k in range(NZ):
                r0 = (2 * k + other) * PAD
                u = xp[r0 : r0 + PAD, cols].astype(F32)[:SH] * ai
                term = ai * (pull[r0 : r0 + SH] - u * sn)
                if k == NZ // 2:
                    ref = outs[at + (n * W) // HALF]
                    c0 = (n * W) % HALF
                    ref[:, c0 : c0 + W] = term.astype(BF16)
                    at += 2
                else:
                    outs[at][:, cols] = term
                    at += 1


def caption_kernel(xp, cx, yp, brow, sj, *outs):
    own, away = outs[:8], outs[8:10]
    xlo, y, core, z, xhi = coords()
    b, s = brow[...], sj[...]
    coeff = cx[...]
    for swapped in range(2):
        for other in range(2):
            for k in range(NY):
                g = (xlo + other) % 2 * 4 + (y + k) % 4
                block = (g - z + NZ) % NZ * 2 + (core + swapped + xhi) % 2
                rows = pl.ds(pl.multiple_of(block * PAD, 16), PAD)
                pull = lax.dot_general(
                    xp[rows, :], coeff, (((1,), (1,)), ((), ())), preferred_element_type=F32
                )
                v = yp[rows, :].astype(F32) * b
                term = (b * (pull - v * s))[:SH]
                if swapped:
                    away[other][k] = term.astype(BF16)
                else:
                    own[other * NY + k][...] = term


def call(kernel, out_shape, flops, args, scratch=(), smem=()):
    vm = pl.BlockSpec(memory_space=pltpu.VMEM)
    specs = [pl.BlockSpec(memory_space=pltpu.SMEM) if i in smem else vm for i in range(len(args))]
    moved = sum(x.size * x.dtype.itemsize for x in list(args) + list(out_shape))
    return pl.pallas_call(
        kernel,
        out_shape=out_shape,
        in_specs=specs,
        out_specs=[vm] * len(out_shape),
        scratch_shapes=list(scratch),
        compiler_params=pltpu.CompilerParams(vmem_limit_bytes=VMEM_LIMIT),
        cost_estimate=pl.CostEstimate(flops=flops, bytes_accessed=moved, transcendentals=0),
    )(*args)


def flat(ring, n):
    return [p for k in range(n) for p in ring[k]]


def sds(shape, dtype):
    return jax.ShapeDtypeStruct(shape, dtype)


def wide(v):
    return v.astype(F32)


def left(r):
    return jnp.pad(wide(r), ((0, 0), (0, HALF)))


def right(r):
    return jnp.pad(wide(r), ((0, 0), (HALF, 0)))


def ring_sum(terms, halves, shift, n):
    half = n // 2
    up = left(shift(halves[0], 1))
    down = right(shift(halves[1], -1))
    for k in range(half - 1, 0, -1):
        up = shift((terms[k] + wide(up)).astype(BF16), 1)
        down = shift((terms[n - k] + wide(down)).astype(BF16), -1)
    return terms[0] + wide(up) + wide(down)


def shards(images, texts, pairs, log_scale, bias):
    txt = [ring_gather(texts, shift_y, NY), ring_gather(swap_xlo(texts), shift_y, NY)]
    img = [ring_gather(images, shift_z, NZ), ring_gather(swap_xhi(images), shift_z, NZ)]
    own = flat(txt[0], NY) + flat(txt[1], NY)
    yp, ypt, brow, bcol = call(
        text_kernel,
        [sds((ROWS, N), BF16), sds((N, ROWS), BF16), sds((1, N), F32), sds((N, 128), F32)],
        2 * 1024 * 1024 * 64,
        own + [swap_core(p) for p in own],
    )
    shapes = [sds((ROWS, N), BF16), sds((N, N), BF16), sds((1, N), F32), sds((1, N), F32)]
    for _ in range(2):
        for k in range(NZ):
            shapes += [sds((SH, HALF), BF16)] * 2 if k == NZ // 2 else [sds((SH, N), F32)]
    args = flat(img[0], NZ) + flat(img[1], NZ)
    res = call(
        image_kernel,
        shapes,
        4 * N * N * ROWS,
        args + [pairs.reshape(1, N), log_scale, bias, yp, ypt, bcol],
        [
            pltpu.VMEM((N, N), F32),
            pltpu.VMEM((N, N), BF16),
            pltpu.VMEM((8, N), F32),
            pltpu.VMEM((8, N), F32),
            pltpu.VMEM((N, 128), F32),
        ],
        smem=(19, 20),
    )
    xp, cx, sj, loss = res[:4]
    sums = []
    for other in range(2):
        part = list(res[4 + 9 * other : 13 + 9 * other])
        halves = part[4:6]
        terms = part[:4] + [None] + part[6:]
        sums.append((terms, halves))
    far = ring_sum(sums[1][0], sums[1][1], shift_z, NZ)
    near = ring_sum(sums[0][0], sums[0][1], shift_z, NZ)
    image_grad = near + wide(swap_xhi(far.astype(BF16)))

    cap = call(
        caption_kernel,
        [sds((SH, N), F32)] * 8 + [sds((NY, SH, N), BF16)] * 2,
        2 * N * N * ROWS,
        [xp, cx, yp, brow, sj],
    )
    sides = []
    for other in (1, 0):
        got = swap_core(cap[8 + other])
        terms = [cap[other * NY + k] + wide(got[k]) for k in range(NY)]
        middle = terms[NY // 2].astype(BF16)
        sides.append(ring_sum(terms, (middle[:, :HALF], middle[:, HALF:]), shift_y, NY))
    text_grad = sides[1] + wide(swap_xlo(sides[0].astype(BF16)))

    total = loss.reshape(8, 128)
    total = total + swap_xhi(total)
    for b in (1, 2, 4):
        total = total + xor_z(total, b)
    return (total.reshape(N), image_grad, text_grad)


def solution(mesh):
    return jax.shard_map(
        shards,
        mesh=mesh,
        in_specs=(P("col", "row"), P("row", "col"), P("row"), P(), P()),
        out_specs=(P("row"), P("col", "row"), P("row", "col")),
        check_vma=False,
    )
```

```python
import jax
import jax.numpy as jnp
from jax import lax
from jax.experimental import pallas as pl
from jax.experimental.pallas import tpu as pltpu
from jax.sharding import PartitionSpec as P

EPS = 1e-06
F32 = jnp.float32
BF16 = jnp.bfloat16
NZ, NY = 8, 4
SH = 72
BL = 2 * SH
N = 1024
HALF = N // 2
ROWS = 16 * SH
MIB = 1024 * 1024


def row_pairs(f):
    out = []
    for r in range(16):
        a, b, c = f(r // 8, (r // 2) % 4, r % 2)
        out.append((r, (a * 4 + b) * 2 + c))
    return out


def col_pairs(f):
    out = []
    for r in range(16):
        a, b = f(r // 2, r % 2)
        out.append((r, a * 2 + b))
    return out


def shift_z(v, d):
    return lax.ppermute(v, "col", col_pairs(lambda z, h: ((z + d) % NZ, h)))


def shift_y(v, d):
    return lax.ppermute(v, "row", row_pairs(lambda x, y, c: (x, (y + d) % NY, c)))


def swap_xhi(v):
    return lax.ppermute(v, "col", col_pairs(lambda z, h: (z, 1 - h)))


def swap_xlo(v):
    return lax.ppermute(v, "row", row_pairs(lambda x, y, c: (1 - x, y, c)))


def swap_core(v):
    return lax.ppermute(v, "row", row_pairs(lambda x, y, c: (x, y, 1 - c)))


def coords():
    row, col = lax.axis_index("row"), lax.axis_index("col")
    return row // 8, (row // 2) % 4, row % 2, col // 2, col % 2


def halves(v):
    return v[:SH], v[SH:]


def text_kernel(*refs):
    mine, others = refs[:4], refs[4]
    yp, ypt, brow, bcol = refs[5:]
    xlo, y, core, z, xhi = coords()
    same = core == xhi
    total = jnp.zeros((1, N), F32)
    for k in range(NY):
        here = halves(mine[k][...].astype(F32))
        away = halves(others[k].astype(F32))
        for other in range(2):
            a, b = here[other], away[other]
            block = jnp.concatenate([jnp.where(same, a, b), jnp.where(same, b, a)], axis=0)
            g = (xlo + other) % 2 * 4 + (y + k) % 4
            at = (g - z + NZ) % NZ * BL
            yp[pl.ds(pl.multiple_of(at, BL), BL), :] = block.astype(BF16)
            total += jnp.sum(block * block, axis=0, keepdims=True)
    brow[...] = lax.rsqrt(total + EPS)
    for c in range(N // 128):
        v = yp[:, c * 128 : (c + 1) * 128].T
        ypt[c * 128 : (c + 1) * 128, :] = v
        w = v.astype(F32)
        s = jnp.sum(w * w, axis=1, keepdims=True)
        bcol[c * 128 : (c + 1) * 128, :] = jnp.broadcast_to(lax.rsqrt(s + EPS), (128, 128))


LANES = 128
TILE = 64


def image_kernel(*refs):
    pieces = refs[:9]
    pairs, logscale, bias, yp, ypt, bcol = refs[9:15]
    xp, cx, sj, loss = refs[15:19]
    outs = refs[19:28]
    t_ref, cy, acc_sj = refs[28:]
    total = jnp.zeros((1, N), F32)
    at = 0
    for k in range(NZ):
        rows = slice(k * BL, (k + 1) * BL)
        if k == NZ // 2:
            xp[rows, :HALF] = pieces[at][...]
            xp[rows, HALF:] = pieces[at + 1][...]
            at += 2
        else:
            xp[rows, :] = pieces[at][...]
            at += 1
        v = xp[rows, :].astype(F32)
        total += jnp.sum(v * v, axis=0, keepdims=True)
    a = lax.rsqrt(total + EPS)
    scale = jnp.exp(jnp.full((1, N), logscale[0], F32))
    ascale = a * scale
    shift = bias[0]
    acc_sj[...] = jnp.zeros_like(acc_sj)
    first = lax.axis_index("col") * N
    W = 256
    for n in range(N // W):
        t_ref[:, n * W : (n + 1) * W] = jnp.dot(
            ypt[...], xp[:, n * W : (n + 1) * W], preferred_element_type=F32
        )
    sub = TILE // 8
    losses, inners = [], []
    for n in range(N // LANES):
        cols = slice(n * LANES, (n + 1) * LANES)
        ai, asc, sc, pair = a[:, cols], ascale[:, cols], scale[:, cols], pairs[:, cols] - first

        def body(j, carry, cols=cols, ai=ai, asc=asc, sc=sc, pair=pair):
            al, asi = carry
            rows = pl.ds(pl.multiple_of(j * TILE, TILE), TILE)
            b = bcol[rows, :]
            cos = (t_ref[rows, cols] * b) * ai
            logit = cos * sc + shift
            ids = lax.broadcasted_iota(jnp.int32, (TILE, LANES), 0)
            hit = ids == pair - j * TILE
            e = jnp.exp(logit)
            sig = e * pl.reciprocal(1.0 + e)
            d = jnp.where(hit, sig - 1.0, sig)
            dc = d * cos
            cy[rows, cols] = ((d * b) * sc).astype(BF16)
            cx[rows, cols] = (d * asc).astype(BF16)
            acc_sj[rows, :] += dc
            e8 = e.reshape(sub, 8, LANES)
            q = e8[0]
            for m in range(1, sub):
                q = q + (e8[m] + q * e8[m])
            soft = jnp.where(q < 1e-4, (1.0 - 0.5 * q) * q, jnp.log(1.0 + q))
            al = al + soft - jnp.sum(jnp.where(hit, logit, 0.0).reshape(sub, 8, LANES), axis=0)
            asi = asi + jnp.sum(dc.reshape(sub, 8, LANES), axis=0)
            return al, asi

        zero = jnp.zeros((8, LANES), F32)
        al, asi = lax.fori_loop(0, N // TILE, body, (zero, zero))
        losses.append(jnp.sum(al, axis=0, keepdims=True))
        inners.append(jnp.sum(asi, axis=0, keepdims=True) * sc)
    loss[...] = jnp.concatenate(losses, axis=1)
    sj[...] = jnp.sum(acc_sj[...].T, axis=0, keepdims=True) * scale
    si = jnp.concatenate(inners, axis=1)
    for n in range(N // W):
        cols = slice(n * W, (n + 1) * W)
        pull = jnp.dot(yp[...], cy[:, cols], preferred_element_type=F32)
        ai, sn = a[:, cols], si[:, cols]
        at = 0
        for k in range(NZ):
            rows = slice(k * BL, (k + 1) * BL)
            u = xp[rows, cols].astype(F32) * ai
            term = ai * (pull[rows] - u * sn)
            if k == NZ // 2:
                c0 = (n * W) % HALF
                outs[at + (n * W) // HALF][:, c0 : c0 + W] = term.astype(BF16)
                at += 2
            else:
                outs[at][:, cols] = term
                at += 1


def caption_kernel(xp, cx, yp, brow, sj, *refs):
    own, away = refs[:4], refs[4]
    t_ref = refs[5]
    xlo, y, core, z, xhi = coords()
    same = core == xhi
    W = 256
    for n in range(N // W):
        cols = slice(n * W, (n + 1) * W)
        pull = lax.dot_general(
            xp[...], cx[cols, :], (((1,), (1,)), ((), ())), preferred_element_type=F32
        )
        b, s = brow[:, cols], sj[:, cols]
        t_ref[:, cols] = b * (pull - (yp[:, cols].astype(F32) * b) * s)
    for k in range(NY):
        here, there = [], []
        for other in range(2):
            g = (xlo + other) % 2 * 4 + (y + k) % 4
            at = (g - z + NZ) % NZ * BL
            p, q = halves(t_ref[pl.ds(pl.multiple_of(at, BL), BL), :])
            here.append(jnp.where(same, p, q))
            there.append(jnp.where(same, q, p))
        own[k][...] = jnp.concatenate(here, axis=0)
        away[k] = jnp.concatenate(there, axis=0).astype(BF16)


def call(kernel, out_shape, flops, args, scratch=(), smem=(), limit=32 * MIB):
    vm = pl.BlockSpec(memory_space=pltpu.VMEM)
    specs = [pl.BlockSpec(memory_space=pltpu.SMEM) if i in smem else vm for i in range(len(args))]
    moved = sum(x.size * x.dtype.itemsize for x in list(args) + list(out_shape))
    return pl.pallas_call(
        kernel,
        out_shape=out_shape,
        in_specs=specs,
        out_specs=[vm] * len(out_shape),
        scratch_shapes=list(scratch),
        compiler_params=pltpu.CompilerParams(vmem_limit_bytes=limit),
        cost_estimate=pl.CostEstimate(flops=flops, bytes_accessed=moved, transcendentals=0),
    )(*args)


def sds(shape, dtype):
    return jax.ShapeDtypeStruct(shape, dtype)


def wide(v):
    return v.astype(F32)


def run_text(mine, others):
    return call(
        text_kernel,
        [sds((ROWS, N), BF16), sds((N, ROWS), BF16), sds((1, N), F32), sds((N, 128), F32)],
        N * N * 64,
        list(mine) + [others],
    )


def run_image(pieces, pairs, log_scale, bias, yp, ypt, bcol):
    shapes = [sds((ROWS, N), BF16), sds((N, N), BF16), sds((1, N), F32), sds((1, N), F32)]
    for k in range(NZ):
        shapes += [sds((BL, HALF), BF16)] * 2 if k == NZ // 2 else [sds((BL, N), F32)]
    return call(
        image_kernel,
        shapes,
        4 * N * N * ROWS,
        list(pieces) + [pairs.reshape(1, N), log_scale, bias, yp, ypt, bcol],
        [pltpu.VMEM((N, N), F32), pltpu.VMEM((N, N), BF16), pltpu.VMEM((N, 128), F32)],
        smem=(10, 11),
    )


def run_caption(xp, cx, yp, brow, sj):
    return call(
        caption_kernel,
        [sds((BL, N), F32)] * NY + [sds((NY, BL, N), BF16)],
        2 * N * N * ROWS,
        [xp, cx, yp, brow, sj],
        [pltpu.VMEM((ROWS, N), F32)],
    )


def shards(images, texts, pairs, log_scale, bias):
    block = jnp.concatenate([texts, swap_xlo(texts)], axis=0)
    behind = shift_y(block, 1)
    ahead = shift_y(block, -1)
    across = shift_y(behind, 1)
    mine = [block, ahead, across, behind]
    yp, ypt, brow, bcol = run_text(mine, swap_core(jnp.stack(mine)))

    up = down = jnp.concatenate([images, swap_xhi(images)], axis=0)
    ring = [[] for _ in range(NZ)]
    ring[0] = [up]
    for k in range(1, NZ // 2):
        up, down = shift_z(up, 1), shift_z(down, -1)
        ring[NZ - k], ring[k] = [up], [down]
    ring[NZ // 2] = [shift_z(up[:, :HALF], 1), shift_z(down[:, HALF:], -1)]
    res = run_image([p for r in ring for p in r], pairs, log_scale, bias, yp, ypt, bcol)
    xp, cx, sj, loss = res[:4]
    terms = list(res[4:8]) + [None] + list(res[10:13])

    up = jnp.pad(wide(shift_z(res[8], 1)), ((0, 0), (0, HALF)))
    down = jnp.pad(wide(shift_z(res[9], -1)), ((0, 0), (HALF, 0)))
    for k in range(NZ // 2 - 1, 0, -1):
        up = shift_z((terms[k] + wide(up)).astype(BF16), 1)
        down = shift_z((terms[NZ - k] + wide(down)).astype(BF16), -1)
    total = terms[0] + wide(up) + wide(down)
    image_grad = total[:SH] + wide(swap_xhi(total[SH:].astype(BF16)))

    cap = run_caption(xp, cx, yp, brow, sj)
    got = swap_core(cap[NY])
    part = [cap[k] + wide(got[k]) for k in range(NY)]
    up = shift_y(part[2].astype(BF16), 1)
    down = shift_y(part[3].astype(BF16), -1)
    up = shift_y((part[1] + wide(up)).astype(BF16), 1)
    total = part[0] + wide(up) + wide(down)
    text_grad = total[:SH] + wide(swap_xlo(total[SH:].astype(BF16)))

    row_loss = jnp.sum(lax.all_gather(loss, "col", axis=0, tiled=True), axis=0)
    return (row_loss, image_grad, text_grad)


def solution(mesh):
    return jax.shard_map(
        shards,
        mesh=mesh,
        in_specs=(P("col", "row"), P("row", "col"), P("row"), P(), P()),
        out_specs=(P("row"), P("col", "row"), P("row", "col")),
        check_vma=False,
    )
```

```python
import jax
import jax.numpy as jnp
from jax import lax
from jax.experimental import pallas as pl
from jax.experimental.pallas import tpu as pltpu
from jax.sharding import PartitionSpec as P

EPS = 1e-06
F32 = jnp.float32
BF16 = jnp.bfloat16
NZ, NY = 8, 4
SH = 72
BL = 2 * SH
N = 1024
HALF = N // 2
ROWS = 16 * SH
MIB = 1024 * 1024


def row_pairs(f):
    out = []
    for r in range(16):
        a, b, c = f(r // 8, (r // 2) % 4, r % 2)
        out.append((r, (a * 4 + b) * 2 + c))
    return out


def col_pairs(f):
    out = []
    for r in range(16):
        a, b = f(r // 2, r % 2)
        out.append((r, a * 2 + b))
    return out


def shift_z(v, d):
    return lax.ppermute(v, "col", col_pairs(lambda z, h: ((z + d) % NZ, h)))


def shift_y(v, d):
    return lax.ppermute(v, "row", row_pairs(lambda x, y, c: (x, (y + d) % NY, c)))


def swap_xhi(v):
    return lax.ppermute(v, "col", col_pairs(lambda z, h: (z, 1 - h)))


def swap_xlo(v):
    return lax.ppermute(v, "row", row_pairs(lambda x, y, c: (1 - x, y, c)))


def swap_core(v):
    return lax.ppermute(v, "row", row_pairs(lambda x, y, c: (x, y, 1 - c)))


def xor_z(v, b):
    return lax.ppermute(v, "col", col_pairs(lambda z, h: (z ^ b, h)))


def coords():
    row, col = lax.axis_index("row"), lax.axis_index("col")
    return row // 8, (row // 2) % 4, row % 2, col // 2, col % 2


def halves(v):
    return v[:SH], v[SH:]


def text_kernel(*refs):
    mine, others = refs[:4], refs[4]
    yp, ypt, brow, bcol = refs[5:]
    xlo, y, core, z, xhi = coords()
    same = core == xhi
    total = jnp.zeros((1, N), F32)
    for k in range(NY):
        here = halves(mine[k][...].astype(F32))
        away = halves(others[k].astype(F32))
        for other in range(2):
            a, b = here[other], away[other]
            block = jnp.concatenate([jnp.where(same, a, b), jnp.where(same, b, a)], axis=0)
            g = (xlo + other) % 2 * 4 + (y + k) % 4
            at = (g - z + NZ) % NZ * BL
            yp[pl.ds(pl.multiple_of(at, BL), BL), :] = block.astype(BF16)
            total += jnp.sum(block * block, axis=0, keepdims=True)
    brow[...] = lax.rsqrt(total + EPS)
    for c in range(N // 128):
        v = yp[:, c * 128 : (c + 1) * 128].T
        ypt[c * 128 : (c + 1) * 128, :] = v
        w = v.astype(F32)
        s = jnp.sum(w * w, axis=1, keepdims=True)
        bcol[c * 128 : (c + 1) * 128, :] = jnp.broadcast_to(lax.rsqrt(s + EPS), (128, 128))


LANES = 128
TILE = 64


def image_kernel(*refs):
    pieces = refs[:9]
    pairs, logscale, bias, yp, ypt, bcol = refs[9:15]
    xp, cx, sj, loss = refs[15:19]
    outs = refs[19:28]
    t_ref, cy, acc_sj = refs[28:]
    total = jnp.zeros((1, N), F32)
    at = 0
    for k in range(NZ):
        rows = slice(k * BL, (k + 1) * BL)
        if k == NZ // 2:
            xp[rows, :HALF] = pieces[at][...]
            xp[rows, HALF:] = pieces[at + 1][...]
            at += 2
        else:
            xp[rows, :] = pieces[at][...]
            at += 1
        v = xp[rows, :].astype(F32)
        total += jnp.sum(v * v, axis=0, keepdims=True)
    a = lax.rsqrt(total + EPS)
    scale = jnp.exp(jnp.full((1, N), logscale[0], F32))
    ascale = a * scale
    shift = bias[0]
    acc_sj[...] = jnp.zeros_like(acc_sj)
    first = lax.axis_index("col") * N
    W = 256
    for n in range(N // W):
        t_ref[:, n * W : (n + 1) * W] = jnp.dot(
            ypt[...], xp[:, n * W : (n + 1) * W], preferred_element_type=F32
        )
    sub = TILE // 8
    losses, inners = [], []
    for n in range(N // LANES):
        cols = slice(n * LANES, (n + 1) * LANES)
        ai, asc, sc, pair = a[:, cols], ascale[:, cols], scale[:, cols], pairs[:, cols] - first

        def body(j, carry, cols=cols, ai=ai, asc=asc, sc=sc, pair=pair):
            al, asi = carry
            rows = pl.ds(pl.multiple_of(j * TILE, TILE), TILE)
            b = bcol[rows, :]
            cos = (t_ref[rows, cols] * b) * ai
            logit = cos * sc + shift
            ids = lax.broadcasted_iota(jnp.int32, (TILE, LANES), 0)
            hit = ids == pair - j * TILE
            e = jnp.exp(logit)
            sig = e * pl.reciprocal(1.0 + e)
            d = jnp.where(hit, sig - 1.0, sig)
            dc = d * cos
            cy[rows, cols] = ((d * b) * sc).astype(BF16)
            cx[rows, cols] = (d * asc).astype(BF16)
            acc_sj[rows, :] += dc
            e8 = e.reshape(sub, 8, LANES)
            q = e8[0]
            for m in range(1, sub):
                q = q + (e8[m] + q * e8[m])
            soft = jnp.where(q < 1e-4, (1.0 - 0.5 * q) * q, jnp.log(1.0 + q))
            al = al + soft - jnp.sum(jnp.where(hit, logit, 0.0).reshape(sub, 8, LANES), axis=0)
            asi = asi + jnp.sum(dc.reshape(sub, 8, LANES), axis=0)
            return al, asi

        zero = jnp.zeros((8, LANES), F32)
        al, asi = lax.fori_loop(0, N // TILE, body, (zero, zero))
        losses.append(jnp.sum(al, axis=0, keepdims=True))
        inners.append(jnp.sum(asi, axis=0, keepdims=True) * sc)
    loss[...] = jnp.concatenate(losses, axis=1)
    sj[...] = jnp.sum(acc_sj[...].T, axis=0, keepdims=True) * scale
    si = jnp.concatenate(inners, axis=1)
    for n in range(N // W):
        cols = slice(n * W, (n + 1) * W)
        pull = jnp.dot(yp[...], cy[:, cols], preferred_element_type=F32)
        ai, sn = a[:, cols], si[:, cols]
        at = 0
        for k in range(NZ):
            rows = slice(k * BL, (k + 1) * BL)
            u = xp[rows, cols].astype(F32) * ai
            term = ai * (pull[rows] - u * sn)
            if k == NZ // 2:
                c0 = (n * W) % HALF
                outs[at + (n * W) // HALF][:, c0 : c0 + W] = term.astype(BF16)
                at += 2
            else:
                outs[at][:, cols] = term
                at += 1


def caption_kernel(xp, cx, yp, brow, sj, *refs):
    own, away = refs[:4], refs[4]
    t_ref = refs[5]
    xlo, y, core, z, xhi = coords()
    same = core == xhi
    W = 256
    for n in range(N // W):
        cols = slice(n * W, (n + 1) * W)
        pull = lax.dot_general(
            xp[...], cx[cols, :], (((1,), (1,)), ((), ())), preferred_element_type=F32
        )
        b, s = brow[:, cols], sj[:, cols]
        t_ref[:, cols] = b * (pull - (yp[:, cols].astype(F32) * b) * s)
    for k in range(NY):
        here, there = [], []
        for other in range(2):
            g = (xlo + other) % 2 * 4 + (y + k) % 4
            at = (g - z + NZ) % NZ * BL
            p, q = halves(t_ref[pl.ds(pl.multiple_of(at, BL), BL), :])
            here.append(jnp.where(same, p, q))
            there.append(jnp.where(same, q, p))
        own[k][...] = jnp.concatenate(here, axis=0)
        away[k] = jnp.concatenate(there, axis=0).astype(BF16)


def call(kernel, out_shape, flops, args, scratch=(), smem=(), limit=32 * MIB):
    vm = pl.BlockSpec(memory_space=pltpu.VMEM)
    specs = [pl.BlockSpec(memory_space=pltpu.SMEM) if i in smem else vm for i in range(len(args))]
    moved = sum(x.size * x.dtype.itemsize for x in list(args) + list(out_shape))
    return pl.pallas_call(
        kernel,
        out_shape=out_shape,
        in_specs=specs,
        out_specs=[vm] * len(out_shape),
        scratch_shapes=list(scratch),
        compiler_params=pltpu.CompilerParams(vmem_limit_bytes=limit),
        cost_estimate=pl.CostEstimate(flops=flops, bytes_accessed=moved, transcendentals=0),
    )(*args)


def sds(shape, dtype):
    return jax.ShapeDtypeStruct(shape, dtype)


def wide(v):
    return v.astype(F32)


def run_text(mine, others):
    return call(
        text_kernel,
        [sds((ROWS, N), BF16), sds((N, ROWS), BF16), sds((1, N), F32), sds((N, 128), F32)],
        N * N * 64,
        list(mine) + [others],
    )


def run_image(pieces, pairs, log_scale, bias, yp, ypt, bcol):
    shapes = [sds((ROWS, N), BF16), sds((N, N), BF16), sds((1, N), F32), sds((1, N), F32)]
    for k in range(NZ):
        shapes += [sds((BL, HALF), BF16)] * 2 if k == NZ // 2 else [sds((BL, N), F32)]
    return call(
        image_kernel,
        shapes,
        4 * N * N * ROWS,
        list(pieces) + [pairs.reshape(1, N), log_scale, bias, yp, ypt, bcol],
        [pltpu.VMEM((N, N), F32), pltpu.VMEM((N, N), BF16), pltpu.VMEM((N, 128), F32)],
        smem=(10, 11),
    )


def run_caption(xp, cx, yp, brow, sj):
    return call(
        caption_kernel,
        [sds((BL, N), F32)] * NY + [sds((NY, BL, N), BF16)],
        2 * N * N * ROWS,
        [xp, cx, yp, brow, sj],
        [pltpu.VMEM((ROWS, N), F32)],
    )


def together(*values):
    return lax.optimization_barrier(values)


def shards(images, texts, pairs, log_scale, bias):
    other_img, other_txt = together(swap_xhi(images), swap_xlo(texts))
    up = down = jnp.concatenate([images, other_img], axis=0)
    block = jnp.concatenate([texts, other_txt], axis=0)
    ring = [[] for _ in range(NZ)]
    ring[0] = [up]
    up, down, behind, ahead = together(
        shift_z(up, 1), shift_z(down, -1), shift_y(block, 1), shift_y(block, -1)
    )
    ring[NZ - 1], ring[1] = [up], [down]
    up, down, across = together(shift_z(up, 1), shift_z(down, -1), shift_y(behind, 1))
    ring[NZ - 2], ring[2] = [up], [down]
    mine = [block, ahead, across, behind]
    up, down, others = together(shift_z(up, 1), shift_z(down, -1), swap_core(jnp.stack(mine)))
    ring[NZ - 3], ring[3] = [up], [down]
    ring[NZ // 2] = [shift_z(up[:, :HALF], 1), shift_z(down[:, HALF:], -1)]
    yp, ypt, brow, bcol = run_text(mine, others)

    res = run_image([p for r in ring for p in r], pairs, log_scale, bias, yp, ypt, bcol)
    xp, cx, sj, loss = res[:4]
    terms = list(res[4:8]) + [None] + list(res[10:13])
    loss = loss.reshape(8, 128)

    up, down = together(shift_z(res[8], 1), shift_z(res[9], -1))
    lost, xp, cx = together(swap_xhi(loss), xp, cx)
    cap = run_caption(xp, cx, yp, brow, sj)
    loss = loss + lost
    up = jnp.pad(wide(up), ((0, 0), (0, HALF)))
    down = jnp.pad(wide(down), ((0, 0), (HALF, 0)))
    up, down, got, lost = together(
        shift_z((terms[3] + up).astype(BF16), 1),
        shift_z((terms[5] + down).astype(BF16), -1),
        swap_core(cap[NY]),
        xor_z(loss, 1),
    )
    loss = loss + lost
    part = [cap[k] + wide(got[k]) for k in range(NY)]
    up, down, tup, tdown, lost = together(
        shift_z((terms[2] + wide(up)).astype(BF16), 1),
        shift_z((terms[6] + wide(down)).astype(BF16), -1),
        shift_y(part[2].astype(BF16), 1),
        shift_y(part[3].astype(BF16), -1),
        xor_z(loss, 2),
    )
    loss = loss + lost
    up, down, tup, lost = together(
        shift_z((terms[1] + wide(up)).astype(BF16), 1),
        shift_z((terms[7] + wide(down)).astype(BF16), -1),
        shift_y((part[1] + wide(tup)).astype(BF16), 1),
        xor_z(loss, 4),
    )
    loss = loss + lost
    total = terms[0] + wide(up) + wide(down)
    image_grad = total[:SH] + wide(swap_xhi(total[SH:].astype(BF16)))
    total = part[0] + wide(tup) + wide(tdown)
    text_grad = total[:SH] + wide(swap_xlo(total[SH:].astype(BF16)))
    return (loss.reshape(N), image_grad, text_grad)


def solution(mesh):
    return jax.shard_map(
        shards,
        mesh=mesh,
        in_specs=(P("col", "row"), P("row", "col"), P("row"), P(), P()),
        out_specs=(P("row"), P("col", "row"), P("row", "col")),
        check_vma=False,
    )
```

```python
import jax
import jax.numpy as jnp
from jax import lax
from jax.experimental import pallas as pl
from jax.experimental.pallas import tpu as pltpu
from jax.sharding import PartitionSpec as P

EPS = 1e-06
F32 = jnp.float32
BF16 = jnp.bfloat16
NZ, NY = 8, 4
SH = 72
BL = 2 * SH
N = 1024
HALF = N // 2
ROWS = 16 * SH
MIB = 1024 * 1024


def row_pairs(f):
    out = []
    for r in range(16):
        a, b, c = f(r // 8, (r // 2) % 4, r % 2)
        out.append((r, (a * 4 + b) * 2 + c))
    return out


def col_pairs(f):
    out = []
    for r in range(16):
        a, b = f(r // 2, r % 2)
        out.append((r, a * 2 + b))
    return out


def shift_z(v, d):
    return lax.ppermute(v, "col", col_pairs(lambda z, h: ((z + d) % NZ, h)))


def shift_y(v, d):
    return lax.ppermute(v, "row", row_pairs(lambda x, y, c: (x, (y + d) % NY, c)))


def swap_xhi(v):
    return lax.ppermute(v, "col", col_pairs(lambda z, h: (z, 1 - h)))


def swap_xlo(v):
    return lax.ppermute(v, "row", row_pairs(lambda x, y, c: (1 - x, y, c)))


def swap_core(v):
    return lax.ppermute(v, "row", row_pairs(lambda x, y, c: (x, y, 1 - c)))


def xor_z(v, b):
    return lax.ppermute(v, "col", col_pairs(lambda z, h: (z ^ b, h)))


def coords():
    row, col = lax.axis_index("row"), lax.axis_index("col")
    return row // 8, (row // 2) % 4, row % 2, col // 2, col % 2


def halves(v):
    return v[:SH], v[SH:]


def text_kernel(*refs):
    mine, others = refs[:4], refs[4:8]
    yp, ypt, brow, bcol = refs[8:]
    xlo, y, core, z, xhi = coords()
    same = core == xhi
    total = jnp.zeros((1, N), F32)
    for k in range(NY):
        here = halves(mine[k][...].astype(F32))
        away = halves(others[k][...].astype(F32))
        for other in range(2):
            a, b = here[other], away[other]
            block = jnp.concatenate([jnp.where(same, a, b), jnp.where(same, b, a)], axis=0)
            g = (xlo + other) % 2 * 4 + (y + k) % 4
            at = (g - z + NZ) % NZ * BL
            yp[pl.ds(pl.multiple_of(at, BL), BL), :] = block.astype(BF16)
            total += jnp.sum(block * block, axis=0, keepdims=True)
    brow[...] = lax.rsqrt(total + EPS)
    for c in range(N // 128):
        v = yp[:, c * 128 : (c + 1) * 128].T
        ypt[c * 128 : (c + 1) * 128, :] = v
        w = v.astype(F32)
        s = jnp.sum(w * w, axis=1, keepdims=True)
        bcol[c * 128 : (c + 1) * 128, :] = jnp.broadcast_to(lax.rsqrt(s + EPS), (128, 128))


LANES = 128
TILE = 64


def image_kernel(*refs):
    pieces = refs[:9]
    pairs, logscale, bias, yp, ypt, bcol = refs[9:15]
    xp, cx, sj, loss = refs[15:19]
    outs = refs[19:28]
    t_ref, cy, acc_sj = refs[28:]
    total = jnp.zeros((1, N), F32)
    at = 0
    for k in range(NZ):
        rows = slice(k * BL, (k + 1) * BL)
        if k == NZ // 2:
            xp[rows, :HALF] = pieces[at][...]
            xp[rows, HALF:] = pieces[at + 1][...]
            at += 2
        else:
            xp[rows, :] = pieces[at][...]
            at += 1
        v = xp[rows, :].astype(F32)
        total += jnp.sum(v * v, axis=0, keepdims=True)
    a = lax.rsqrt(total + EPS)
    scale = jnp.exp(jnp.full((1, N), logscale[0], F32))
    ascale = a * scale
    shift = bias[0]
    acc_sj[...] = jnp.zeros_like(acc_sj)
    first = lax.axis_index("col") * N
    W = 256
    for n in range(N // W):
        t_ref[:, n * W : (n + 1) * W] = jnp.dot(
            ypt[...], xp[:, n * W : (n + 1) * W], preferred_element_type=F32
        )
    sub = TILE // 8
    losses, inners = [], []
    for n in range(N // LANES):
        cols = slice(n * LANES, (n + 1) * LANES)
        ai, asc, sc, pair = a[:, cols], ascale[:, cols], scale[:, cols], pairs[:, cols] - first

        def body(j, carry, cols=cols, ai=ai, asc=asc, sc=sc, pair=pair):
            al, asi = carry
            rows = pl.ds(pl.multiple_of(j * TILE, TILE), TILE)
            b = bcol[rows, :]
            cos = (t_ref[rows, cols] * b) * ai
            logit = cos * sc + shift
            ids = lax.broadcasted_iota(jnp.int32, (TILE, LANES), 0)
            hit = ids == pair - j * TILE
            e = jnp.exp(logit)
            sig = e * pl.reciprocal(1.0 + e)
            d = jnp.where(hit, sig - 1.0, sig)
            dc = d * cos
            cy[rows, cols] = ((d * b) * sc).astype(BF16)
            cx[rows, cols] = (d * asc).astype(BF16)
            acc_sj[rows, :] += dc
            e8 = e.reshape(sub, 8, LANES)
            q = e8[0]
            for m in range(1, sub):
                q = q + (e8[m] + q * e8[m])
            soft = jnp.where(q < 1e-4, (1.0 - 0.5 * q) * q, jnp.log(1.0 + q))
            al = al + soft - jnp.sum(jnp.where(hit, logit, 0.0).reshape(sub, 8, LANES), axis=0)
            asi = asi + jnp.sum(dc.reshape(sub, 8, LANES), axis=0)
            return al, asi

        zero = jnp.zeros((8, LANES), F32)
        al, asi = lax.fori_loop(0, N // TILE, body, (zero, zero))
        losses.append(jnp.sum(al, axis=0, keepdims=True))
        inners.append(jnp.sum(asi, axis=0, keepdims=True) * sc)
    loss[...] = jnp.concatenate(losses, axis=1)
    sj[...] = jnp.sum(acc_sj[...].T, axis=0, keepdims=True) * scale
    si = jnp.concatenate(inners, axis=1)
    for n in range(N // W):
        cols = slice(n * W, (n + 1) * W)
        pull = jnp.dot(yp[...], cy[:, cols], preferred_element_type=F32)
        ai, sn = a[:, cols], si[:, cols]
        at = 0
        for k in range(NZ):
            rows = slice(k * BL, (k + 1) * BL)
            u = xp[rows, cols].astype(F32) * ai
            term = ai * (pull[rows] - u * sn)
            if k == NZ // 2:
                c0 = (n * W) % HALF
                outs[at + (n * W) // HALF][:, c0 : c0 + W] = term.astype(BF16)
                at += 2
            else:
                outs[at][:, cols] = term
                at += 1


def caption_kernel(xp, cx, yp, brow, sj, *refs):
    own, away = refs[:4], refs[4:8]
    t_ref = refs[8]
    xlo, y, core, z, xhi = coords()
    same = core == xhi
    W = 256
    for n in range(N // W):
        cols = slice(n * W, (n + 1) * W)
        pull = lax.dot_general(
            xp[...], cx[cols, :], (((1,), (1,)), ((), ())), preferred_element_type=F32
        )
        b, s = brow[:, cols], sj[:, cols]
        t_ref[:, cols] = b * (pull - (yp[:, cols].astype(F32) * b) * s)
    for k in range(NY):
        here, there = [], []
        for other in range(2):
            g = (xlo + other) % 2 * 4 + (y + k) % 4
            at = (g - z + NZ) % NZ * BL
            p, q = halves(t_ref[pl.ds(pl.multiple_of(at, BL), BL), :])
            here.append(jnp.where(same, p, q))
            there.append(jnp.where(same, q, p))
        own[k][...] = jnp.concatenate(here, axis=0)
        away[k][...] = jnp.concatenate(there, axis=0).astype(BF16)


def call(kernel, out_shape, flops, args, scratch=(), smem=(), limit=32 * MIB):
    vm = pl.BlockSpec(memory_space=pltpu.VMEM)
    specs = [pl.BlockSpec(memory_space=pltpu.SMEM) if i in smem else vm for i in range(len(args))]
    moved = sum(x.size * x.dtype.itemsize for x in list(args) + list(out_shape))
    return pl.pallas_call(
        kernel,
        out_shape=out_shape,
        in_specs=specs,
        out_specs=[vm] * len(out_shape),
        scratch_shapes=list(scratch),
        compiler_params=pltpu.CompilerParams(vmem_limit_bytes=limit),
        cost_estimate=pl.CostEstimate(flops=flops, bytes_accessed=moved, transcendentals=0),
    )(*args)


def sds(shape, dtype):
    return jax.ShapeDtypeStruct(shape, dtype)


def wide(v):
    return v.astype(F32)


def run_text(mine, others):
    return call(
        text_kernel,
        [sds((ROWS, N), BF16), sds((N, ROWS), BF16), sds((1, N), F32), sds((N, 128), F32)],
        N * N * 64,
        list(mine) + list(others),
    )


def run_image(pieces, pairs, log_scale, bias, yp, ypt, bcol):
    shapes = [sds((ROWS, N), BF16), sds((N, N), BF16), sds((1, N), F32), sds((1, N), F32)]
    for k in range(NZ):
        shapes += [sds((BL, HALF), BF16)] * 2 if k == NZ // 2 else [sds((BL, N), F32)]
    return call(
        image_kernel,
        shapes,
        4 * N * N * ROWS,
        list(pieces) + [pairs.reshape(1, N), log_scale, bias, yp, ypt, bcol],
        [pltpu.VMEM((N, N), F32), pltpu.VMEM((N, N), BF16), pltpu.VMEM((N, 128), F32)],
        smem=(10, 11),
    )


def run_caption(xp, cx, yp, brow, sj):
    return call(
        caption_kernel,
        [sds((BL, N), F32)] * NY + [sds((BL, N), BF16)] * NY,
        2 * N * N * ROWS,
        [xp, cx, yp, brow, sj],
        [pltpu.VMEM((ROWS, N), F32)],
    )


def after(value, *earlier):
    return lax.optimization_barrier((value, *earlier))[0]


def shards(images, texts, pairs, log_scale, bias):
    other_img, other_txt = swap_xhi(images), swap_xlo(texts)
    up = down = jnp.concatenate([images, other_img], axis=0)
    block = jnp.concatenate([texts, other_txt], axis=0)
    ring = [[] for _ in range(NZ)]
    ring[0] = [up]
    block = after(block, other_img)
    behind, ahead = shift_y(block, 1), shift_y(block, -1)
    others = [swap_core(block)]
    up, down = shift_z(up, 1), shift_z(down, -1)
    ring[NZ - 1], ring[1] = [up], [down]
    behind, ahead = after(behind, up, down), after(ahead, up, down)
    across = shift_y(behind, 1)
    others += [swap_core(ahead)]
    last = swap_core(behind)
    up, down = shift_z(up, 1), shift_z(down, -1)
    ring[NZ - 2], ring[2] = [up], [down]
    across = after(across, up, down)
    others += [swap_core(across), last]
    mine = [block, ahead, across, behind]
    up, down = shift_z(up, 1), shift_z(down, -1)
    ring[NZ - 3], ring[3] = [up], [down]
    mine[0] = after(block, up, down)
    ring[NZ // 2] = [shift_z(up[:, :HALF], 1), shift_z(down[:, HALF:], -1)]
    yp, ypt, brow, bcol = run_text(mine, others)

    res = run_image([p for r in ring for p in r], pairs, log_scale, bias, yp, ypt, bcol)
    xp, cx, sj, loss = res[:4]
    terms = list(res[4:8]) + [None] + list(res[10:13])
    loss = loss.reshape(8, 128)

    up, down = shift_z(res[8], 1), shift_z(res[9], -1)
    cap = run_caption(xp, cx, yp, brow, sj)
    loss = loss + swap_xhi(loss)
    loss = loss + xor_z(after(loss, up, down), 1)
    got = [swap_core(after(v, up, down)) for v in cap[NY:]]
    up = jnp.pad(wide(up), ((0, 0), (0, HALF)))
    down = jnp.pad(wide(down), ((0, 0), (HALF, 0)))
    up = shift_z((terms[3] + up).astype(BF16), 1)
    down = shift_z((terms[5] + down).astype(BF16), -1)
    loss = loss + xor_z(after(loss, up, down), 2)
    part = [cap[k] + wide(got[k]) for k in range(NY)]
    far, near = after(part[2].astype(BF16), up, down), after(part[3].astype(BF16), up, down)
    tup, tdown = shift_y(far, 1), shift_y(near, -1)
    up = shift_z((terms[2] + wide(up)).astype(BF16), 1)
    down = shift_z((terms[6] + wide(down)).astype(BF16), -1)
    loss = loss + xor_z(after(loss, up, down), 4)
    tup = shift_y(after((part[1] + wide(tup)).astype(BF16), up, down), 1)
    up = shift_z((terms[1] + wide(up)).astype(BF16), 1)
    down = shift_z((terms[7] + wide(down)).astype(BF16), -1)
    total = terms[0] + wide(up) + wide(down)
    image_grad = total[:SH] + wide(swap_xhi(total[SH:].astype(BF16)))
    total = part[0] + wide(tup) + wide(tdown)
    text_grad = total[:SH] + wide(swap_xlo(total[SH:].astype(BF16)))
    return (loss.reshape(N), image_grad, text_grad)


def solution(mesh):
    return jax.shard_map(
        shards,
        mesh=mesh,
        in_specs=(P("col", "row"), P("row", "col"), P("row"), P(), P()),
        out_specs=(P("row"), P("col", "row"), P("row", "col")),
        check_vma=False,
    )
```

```python
import jax
import jax.numpy as jnp
from jax import lax
from jax.experimental import pallas as pl
from jax.experimental.pallas import tpu as pltpu
from jax.sharding import PartitionSpec as P

EPS = 1e-06
F32 = jnp.float32
BF16 = jnp.bfloat16
NZ, NY = 8, 4
SH = 72
BL = 2 * SH
N = 1024
HALF = N // 2
ROWS = 16 * SH
MIB = 1024 * 1024


def row_pairs(f):
    out = []
    for r in range(16):
        a, b, c = f(r // 8, (r // 2) % 4, r % 2)
        out.append((r, (a * 4 + b) * 2 + c))
    return out


def col_pairs(f):
    out = []
    for r in range(16):
        a, b = f(r // 2, r % 2)
        out.append((r, a * 2 + b))
    return out


def shift_z(v, d):
    return lax.ppermute(v, "col", col_pairs(lambda z, h: ((z + d) % NZ, h)))


def shift_y(v, d):
    return lax.ppermute(v, "row", row_pairs(lambda x, y, c: (x, (y + d) % NY, c)))


def swap_xhi(v):
    return lax.ppermute(v, "col", col_pairs(lambda z, h: (z, 1 - h)))


def swap_xlo(v):
    return lax.ppermute(v, "row", row_pairs(lambda x, y, c: (1 - x, y, c)))


def swap_core(v):
    return lax.ppermute(v, "row", row_pairs(lambda x, y, c: (x, y, 1 - c)))


def xor_z(v, b):
    return lax.ppermute(v, "col", col_pairs(lambda z, h: (z ^ b, h)))


def coords():
    row, col = lax.axis_index("row"), lax.axis_index("col")
    return row // 8, (row // 2) % 4, row % 2, col // 2, col % 2


def halves(v):
    return v[:SH], v[SH:]


def position(k):
    return jnp.where(k < 4, k, jnp.where(k == 4, 7, k - 1))


ORDER = (0, 1, 2, 3, 5, 6, 7, 4)
EARLY = 7 * BL
WIDE = 1024
TAIL = 896


def text_kernel(*refs):
    mine, others = refs[:4], refs[4:8]
    yp, ypt, brow, bcol = refs[8:]
    xlo, y, core, z, xhi = coords()
    same = core == xhi
    total = jnp.zeros((1, N), F32)
    for k in range(NY):
        here = halves(mine[k][...].astype(F32))
        away = halves(others[k][...].astype(F32))
        for other in range(2):
            a, b = here[other], away[other]
            block = jnp.concatenate([jnp.where(same, a, b), jnp.where(same, b, a)], axis=0)
            g = (xlo + other) % 2 * 4 + (y + k) % 4
            at = position((g - z + NZ) % NZ) * BL
            yp[pl.ds(pl.multiple_of(at, BL), BL), :] = block.astype(BF16)
            total += jnp.sum(block * block, axis=0, keepdims=True)
    brow[...] = lax.rsqrt(total + EPS)
    for c in range(N // 128):
        v = yp[:, c * 128 : (c + 1) * 128].T
        ypt[c * 128 : (c + 1) * 128, :] = v
        w = v.astype(F32)
        s = jnp.sum(w * w, axis=1, keepdims=True)
        bcol[c * 128 : (c + 1) * 128, :] = jnp.broadcast_to(lax.rsqrt(s + EPS), (128, 128))


W = 256


def early_kernel(*refs):
    blocks, ypt = refs[:7], refs[7]
    xa, part, square = refs[8:]
    total = jnp.zeros((1, N), F32)
    for i, block in enumerate(blocks):
        v = block[...]
        xa[i * BL : (i + 1) * BL, :] = v
        v = v.astype(F32)
        total += jnp.sum(v * v, axis=0, keepdims=True)
    xa[EARLY:, :] = jnp.zeros((WIDE - EARLY, N), BF16)
    square[...] = total
    for n in range(N // W):
        cols = slice(n * W, (n + 1) * W)
        part[:, cols] = jnp.dot(ypt[:, :WIDE], xa[:, cols], preferred_element_type=F32)


LANES = 512
TILE = 64


def middle_kernel(
    left, right, part, square, pairs, logscale, bias, yp, ypt, bcol,
    x4, cy, cx, sj, si, arow, loss, out_left, out_right, xb, t_ref, acc_sj,
):
    x4[:, :HALF] = left[...]
    x4[:, HALF:] = right[...]
    xb[: EARLY - TAIL, :] = jnp.zeros((EARLY - TAIL, N), BF16)
    xb[EARLY - TAIL :, :] = x4[...]
    v = x4[...].astype(F32)
    a = lax.rsqrt(square[...] + jnp.sum(v * v, axis=0, keepdims=True) + EPS)
    arow[...] = a
    scale = jnp.exp(jnp.full((1, N), logscale[0], F32))
    ascale = a * scale
    shift = bias[0]
    acc_sj[...] = jnp.zeros_like(acc_sj)
    first = lax.axis_index("col") * N
    sub = TILE // 8
    strips = LANES // 128
    for n in range(N // LANES):
        cols = slice(n * LANES, (n + 1) * LANES)
        t_ref[...] = jnp.dot(ypt[:, TAIL:], xb[:, cols], preferred_element_type=F32)
        ai, asc, sc, pair = a[:, cols], ascale[:, cols], scale[:, cols], pairs[:, cols] - first

        def body(j, carry, cols=cols, ai=ai, asc=asc, sc=sc, pair=pair):
            al, asi = carry
            rows = pl.ds(pl.multiple_of(j * TILE, TILE), TILE)
            b = jnp.concatenate([bcol[rows, :]] * strips, axis=1)
            cos = ((t_ref[rows, :] + part[rows, cols]) * b) * ai
            logit = cos * sc + shift
            hit = lax.broadcasted_iota(jnp.int32, (TILE, LANES), 0) == pair - j * TILE
            e = jnp.exp(logit)
            sig = e * pltpu.reciprocal(1.0 + e)
            d = jnp.where(hit, sig - 1.0, sig)
            dc = d * cos
            cy[rows, cols] = ((d * b) * sc).astype(BF16)
            cx[rows, cols] = (d * asc).astype(BF16)
            strip = dc[:, :128]
            for m in range(1, strips):
                strip = strip + dc[:, m * 128 : (m + 1) * 128]
            acc_sj[rows, :] += strip
            e8 = e.reshape(sub, 8, LANES)
            q = e8[0]
            for m in range(1, sub):
                q = q + (e8[m] + q * e8[m])
            soft = jnp.where(q < 1e-4, (1.0 - 0.5 * q) * q, jnp.log(1.0 + q))
            al = al + soft - jnp.sum(jnp.where(hit, logit, 0.0).reshape(sub, 8, LANES), axis=0)
            asi = asi + jnp.sum(dc.reshape(sub, 8, LANES), axis=0)
            return al, asi

        zero = jnp.zeros((8, LANES), F32)
        al, asi = lax.fori_loop(0, N // TILE, body, (zero, zero))
        loss[:, cols] = jnp.sum(al, axis=0, keepdims=True)
        inner = jnp.sum(asi, axis=0, keepdims=True) * sc
        si[:, cols] = inner
        pull = jnp.dot(yp[EARLY:, :], cy[:, cols], preferred_element_type=F32)
        term = ai * (pull - (x4[:, cols].astype(F32) * ai) * inner)
        out = out_left if n * LANES < HALF else out_right
        at = n * LANES % HALF
        out[:, at : at + LANES] = term.astype(BF16)
    sj[...] = jnp.sum(acc_sj[...].T, axis=0, keepdims=True) * scale


def image_kernel(xa, yp, cy, arow, si, *outs):
    for n in range(N // W):
        cols = slice(n * W, (n + 1) * W)
        pull = jnp.dot(yp[:EARLY, :], cy[:, cols], preferred_element_type=F32)
        a, s = arow[:, cols], si[:, cols]
        for i in range(7):
            rows = slice(i * BL, (i + 1) * BL)
            outs[i][:, cols] = a * (pull[rows] - (xa[rows, cols].astype(F32) * a) * s)


def caption_kernel(xa, x4, cx, yp, brow, sj, loss, _up, _down, *refs):
    own, away = refs[:4], refs[4:8]
    t_ref = refs[9]
    refs[8][...] = loss[...]
    xlo, y, core, z, xhi = coords()
    same = core == xhi
    dims = (((1,), (1,)), ((), ()))
    for n in range(N // W):
        cols = slice(n * W, (n + 1) * W)
        b, s = brow[:, cols], sj[:, cols]
        coeff = cx[cols, :]
        for src, at in ((xa, 0), (x4, EARLY)):
            rows = slice(at, at + (EARLY if at == 0 else BL))
            pull = lax.dot_general(src[: rows.stop - at, :], coeff, dims, preferred_element_type=F32)
            t_ref[rows, cols] = b * (pull - (yp[rows, cols].astype(F32) * b) * s)
    for k in range(NY):
        here, there = [], []
        for other in range(2):
            g = (xlo + other) % 2 * 4 + (y + k) % 4
            at = position((g - z + NZ) % NZ) * BL
            p, q = halves(t_ref[pl.ds(pl.multiple_of(at, BL), BL), :])
            here.append(jnp.where(same, p, q))
            there.append(jnp.where(same, q, p))
        own[k][...] = jnp.concatenate(here, axis=0)
        away[k][...] = jnp.concatenate(there, axis=0).astype(BF16)


def call(kernel, out_shape, flops, args, scratch=(), smem=(), unread=(), limit=32 * MIB):
    vm = pl.BlockSpec(memory_space=pltpu.VMEM)
    specs = [vm] * len(args)
    for i in smem:
        specs[i] = pl.BlockSpec(memory_space=pltpu.SMEM)
    for i in unread:
        specs[i] = pl.BlockSpec(memory_space=pl.ANY)
    moved = sum(x.size * x.dtype.itemsize for x in list(args) + list(out_shape))
    return pl.pallas_call(
        kernel,
        out_shape=out_shape,
        in_specs=specs,
        out_specs=[vm] * len(out_shape),
        scratch_shapes=list(scratch),
        compiler_params=pltpu.CompilerParams(vmem_limit_bytes=limit),
        cost_estimate=pl.CostEstimate(flops=flops, bytes_accessed=moved, transcendentals=0),
    )(*args)


def sds(shape, dtype):
    return jax.ShapeDtypeStruct(shape, dtype)


def wide(v):
    return v.astype(F32)


def run_text(mine, others):
    return call(
        text_kernel,
        [sds((ROWS, N), BF16), sds((N, ROWS), BF16), sds((1, N), F32), sds((N, 128), F32)],
        N * N * 64,
        list(mine) + list(others),
    )


def run_early(blocks, ypt):
    return call(
        early_kernel,
        [sds((WIDE, N), BF16), sds((N, N), F32), sds((1, N), F32)],
        2 * N * N * WIDE,
        list(blocks) + [ypt],
    )


def run_middle(left, right, part, square, pairs, log_scale, bias, yp, ypt, bcol):
    row = sds((1, N), F32)
    return call(
        middle_kernel,
        [sds((BL, N), BF16), sds((N, N), BF16), sds((N, N), BF16), row, row, row, row]
        + [sds((BL, HALF), BF16)] * 2,
        2 * N * N * ROWS,
        [left, right, part, square, pairs.reshape(1, N), log_scale, bias, yp, ypt, bcol],
        [
            pltpu.VMEM((ROWS - TAIL, N), BF16),
            pltpu.VMEM((N, LANES), F32),
            pltpu.VMEM((N, 128), F32),
        ],
        smem=(5, 6),
    )


def run_images(xa, yp, cy, arow, si):
    return call(
        image_kernel, [sds((BL, N), F32)] * 7, 2 * N * N * EARLY, [xa, yp, cy, arow, si]
    )


def run_captions(xa, x4, cx, yp, brow, sj, loss, up, down):
    return call(
        caption_kernel,
        [sds((BL, N), F32)] * NY + [sds((BL, N), BF16)] * NY + [sds((1, N), F32)],
        2 * N * N * ROWS,
        [xa, x4, cx, yp, brow, sj, loss, up, down],
        [pltpu.VMEM((ROWS, N), F32)],
        unread=(7, 8),
    )


def split(v):
    high = lax.reduce_precision(v, 8, 7)
    return high, lax.reduce_precision(v - high, 8, 7)


def shards(images, texts, pairs, log_scale, bias):
    other_img, other_txt = swap_xhi(images), swap_xlo(texts)
    up = down = jnp.concatenate([images, other_img], axis=0)
    block = jnp.concatenate([texts, other_txt], axis=0)
    ring = [[] for _ in range(NZ)]
    ring[0] = [up]
    behind, ahead = shift_y(block, 1), shift_y(block, -1)
    others = [swap_core(block)]
    up, down = shift_z(up, 1), shift_z(down, -1)
    ring[NZ - 1], ring[1] = [up], [down]
    across = shift_y(behind, 1)
    others += [swap_core(ahead)]
    last = swap_core(behind)
    up, down = shift_z(up, 1), shift_z(down, -1)
    ring[NZ - 2], ring[2] = [up], [down]
    others += [swap_core(across), last]
    mine = [block, ahead, across, behind]
    up, down = shift_z(up, 1), shift_z(down, -1)
    ring[NZ - 3], ring[3] = [up], [down]
    left, right = shift_z(up[:, :HALF], 1), shift_z(down[:, HALF:], -1)
    yp, ypt, brow, bcol = run_text(mine, others)
    xa, products, square = run_early([ring[k][0] for k in ORDER[:7]], ypt)

    x4, cy, cx, sj, si, arow, loss, up, down = run_middle(
        left, right, products, square, pairs, log_scale, bias, yp, ypt, bcol
    )
    up, down = shift_z(up, 1), shift_z(down, -1)
    found = run_images(xa, yp, cy, arow, si)
    terms = {k: found[i] for i, k in enumerate(ORDER[:7])}
    up = (terms[3] + jnp.pad(wide(up), ((0, 0), (0, HALF)))).astype(BF16)
    down = (terms[5] + jnp.pad(wide(down), ((0, 0), (HALF, 0)))).astype(BF16)
    cap = run_captions(xa, x4, cx, yp, brow, sj, loss, up, down)
    up, down = shift_z(up, 1), shift_z(down, -1)
    part = [cap[k] + wide(swap_core(cap[NY + k])) for k in range(NY)]
    tup = shift_y(part[2].astype(BF16), 1)
    tdown = shift_y(part[3].astype(BF16), -1)
    up = shift_z((terms[2] + wide(up)).astype(BF16), 1)
    down = shift_z((terms[6] + wide(down)).astype(BF16), -1)
    tup = shift_y((part[1] + wide(tup)).astype(BF16), 1)
    up = shift_z((terms[1] + wide(up)).astype(BF16), 1)
    down = shift_z((terms[7] + wide(down)).astype(BF16), -1)
    total = terms[0] + wide(up) + wide(down)

    loss = cap[2 * NY]
    for b in (1, 2, 4):
        loss = loss + xor_z(loss, b)
    high, low = split(loss)
    rows = jnp.concatenate([high, low, jnp.zeros((6, N), F32)], axis=0)
    got = wide(swap_xhi(jnp.concatenate([total[SH:], rows], axis=0).astype(BF16)))
    image_grad = total[:SH] + got[:SH]
    loss = (high + low) + (got[SH : SH + 1] + got[SH + 1 : SH + 2])
    total = part[0] + wide(tup) + wide(tdown)
    text_grad = total[:SH] + wide(swap_xlo(total[SH:].astype(BF16)))
    return (loss.reshape(N), image_grad, text_grad)


def solution(mesh):
    return jax.shard_map(
        shards,
        mesh=mesh,
        in_specs=(P("col", "row"), P("row", "col"), P("row"), P(), P()),
        out_specs=(P("row"), P("col", "row"), P("row", "col")),
        check_vma=False,
    )
```

```python
import jax
import jax.numpy as jnp
from jax import lax
from jax.experimental import pallas as pl
from jax.experimental.pallas import tpu as pltpu
from jax.sharding import PartitionSpec as P

EPS = 1e-06
F32 = jnp.float32
BF16 = jnp.bfloat16
NZ, NY = 8, 4
SH = 72
BL = 2 * SH
N = 1024
HALF = N // 2
ROWS = 16 * SH
MIB = 1024 * 1024


def row_pairs(f):
    out = []
    for r in range(16):
        a, b, c = f(r // 8, (r // 2) % 4, r % 2)
        out.append((r, (a * 4 + b) * 2 + c))
    return out


def col_pairs(f):
    out = []
    for r in range(16):
        a, b = f(r // 2, r % 2)
        out.append((r, a * 2 + b))
    return out


def shift_z(v, d):
    return lax.ppermute(v, "col", col_pairs(lambda z, h: ((z + d) % NZ, h)))


def shift_y(v, d):
    return lax.ppermute(v, "row", row_pairs(lambda x, y, c: (x, (y + d) % NY, c)))


def swap_xhi(v):
    return lax.ppermute(v, "col", col_pairs(lambda z, h: (z, 1 - h)))


def swap_xlo(v):
    return lax.ppermute(v, "row", row_pairs(lambda x, y, c: (1 - x, y, c)))


def swap_core(v):
    return lax.ppermute(v, "row", row_pairs(lambda x, y, c: (x, y, 1 - c)))


def xor_z(v, b):
    return lax.ppermute(v, "col", col_pairs(lambda z, h: (z ^ b, h)))


def coords():
    row, col = lax.axis_index("row"), lax.axis_index("col")
    return row // 8, (row // 2) % 4, row % 2, col // 2, col % 2


def halves(v):
    return v[:SH], v[SH:]


def position(k):
    return jnp.where(k < 4, k, jnp.where(k == 4, 7, k - 1))


ORDER = (0, 1, 2, 3, 5, 6, 7, 4)
EARLY = 7 * BL
WIDE = 1024
TAIL = 896


def text_kernel(*refs):
    mine, others = refs[:4], refs[4:8]
    yp, ypt, brow, bcol = refs[8:]
    xlo, y, core, z, xhi = coords()
    same = core == xhi
    total = jnp.zeros((1, N), F32)
    for k in range(NY):
        here = halves(mine[k][...].astype(F32))
        away = halves(others[k][...].astype(F32))
        for other in range(2):
            a, b = here[other], away[other]
            block = jnp.concatenate([jnp.where(same, a, b), jnp.where(same, b, a)], axis=0)
            g = (xlo + other) % 2 * 4 + (y + k) % 4
            at = position((g - z + NZ) % NZ) * BL
            yp[pl.ds(pl.multiple_of(at, BL), BL), :] = block.astype(BF16)
            total += jnp.sum(block * block, axis=0, keepdims=True)
    brow[...] = lax.rsqrt(total + EPS)
    for c in range(N // 128):
        v = yp[:, c * 128 : (c + 1) * 128].T
        ypt[c * 128 : (c + 1) * 128, :] = v
        w = v.astype(F32)
        s = jnp.sum(w * w, axis=1, keepdims=True)
        bcol[c * 128 : (c + 1) * 128, :] = jnp.broadcast_to(lax.rsqrt(s + EPS), (128, 128))


W = 256


def early_kernel(*refs):
    blocks, ypt = refs[:7], refs[7]
    xa, part, square = refs[8:]
    total = jnp.zeros((1, N), F32)
    for i, block in enumerate(blocks):
        v = block[...]
        xa[i * BL : (i + 1) * BL, :] = v
        v = v.astype(F32)
        total += jnp.sum(v * v, axis=0, keepdims=True)
    xa[EARLY:, :] = jnp.zeros((WIDE - EARLY, N), BF16)
    square[...] = total
    for n in range(N // W):
        cols = slice(n * W, (n + 1) * W)
        part[:, cols] = jnp.dot(ypt[:, :WIDE], xa[:, cols], preferred_element_type=F32)


LANES = 512
TILE = 64


def middle_kernel(
    left, right, part, square, pairs, logscale, bias, yp, ypt, bcol,
    x4, cy, cx, sj, si, arow, loss, out_left, out_right, xb, t_ref, acc_sj,
):
    x4[:, :HALF] = left[...]
    x4[:, HALF:] = right[...]
    xb[: EARLY - TAIL, :] = jnp.zeros((EARLY - TAIL, N), BF16)
    xb[EARLY - TAIL :, :] = x4[...]
    v = x4[...].astype(F32)
    a = lax.rsqrt(square[...] + jnp.sum(v * v, axis=0, keepdims=True) + EPS)
    arow[...] = a
    scale = jnp.exp(jnp.full((1, N), logscale[0], F32))
    ascale = a * scale
    shift = bias[0]
    acc_sj[...] = jnp.zeros_like(acc_sj)
    first = lax.axis_index("col") * N
    sub = TILE // 8
    strips = LANES // 128
    for n in range(N // LANES):
        cols = slice(n * LANES, (n + 1) * LANES)
        t_ref[...] = jnp.dot(ypt[:, TAIL:], xb[:, cols], preferred_element_type=F32)
        ai, asc, sc, pair = a[:, cols], ascale[:, cols], scale[:, cols], pairs[:, cols] - first

        def body(j, carry, cols=cols, ai=ai, asc=asc, sc=sc, pair=pair):
            al, asi = carry
            rows = pl.ds(pl.multiple_of(j * TILE, TILE), TILE)
            b = jnp.concatenate([bcol[rows, :]] * strips, axis=1)
            cos = ((t_ref[rows, :] + part[rows, cols]) * b) * ai
            logit = cos * sc + shift
            hit = lax.broadcasted_iota(jnp.int32, (TILE, LANES), 0) == pair - j * TILE
            e = jnp.exp(logit)
            sig = e * pltpu.reciprocal(1.0 + e)
            d = jnp.where(hit, sig - 1.0, sig)
            dc = d * cos
            cy[rows, cols] = ((d * b) * sc).astype(BF16)
            cx[rows, cols] = (d * asc).astype(BF16)
            strip = dc[:, :128]
            for m in range(1, strips):
                strip = strip + dc[:, m * 128 : (m + 1) * 128]
            acc_sj[rows, :] += strip
            e8 = e.reshape(sub, 8, LANES)
            q = e8[0]
            for m in range(1, sub):
                q = q + (e8[m] + q * e8[m])
            soft = jnp.where(q < 1e-4, (1.0 - 0.5 * q) * q, jnp.log(1.0 + q))
            al = al + soft - jnp.sum(jnp.where(hit, logit, 0.0).reshape(sub, 8, LANES), axis=0)
            asi = asi + jnp.sum(dc.reshape(sub, 8, LANES), axis=0)
            return al, asi

        zero = jnp.zeros((8, LANES), F32)
        al, asi = lax.fori_loop(0, N // TILE, body, (zero, zero))
        loss[:, cols] = jnp.sum(al, axis=0, keepdims=True)
        inner = jnp.sum(asi, axis=0, keepdims=True) * sc
        si[:, cols] = inner
        pull = jnp.dot(yp[EARLY:, :], cy[:, cols], preferred_element_type=F32)
        term = ai * (pull - (x4[:, cols].astype(F32) * ai) * inner)
        out = out_left if n * LANES < HALF else out_right
        at = n * LANES % HALF
        out[:, at : at + LANES] = term.astype(BF16)
    sj[...] = jnp.sum(acc_sj[...].T, axis=0, keepdims=True) * scale


def image_kernel(xa, yp, cy, arow, si, *outs):
    for n in range(N // W):
        cols = slice(n * W, (n + 1) * W)
        pull = jnp.dot(yp[:EARLY, :], cy[:, cols], preferred_element_type=F32)
        a, s = arow[:, cols], si[:, cols]
        for i in range(7):
            rows = slice(i * BL, (i + 1) * BL)
            outs[i][:, cols] = a * (pull[rows] - (xa[rows, cols].astype(F32) * a) * s)


def caption_kernel(xa, x4, cx, yp, brow, sj, _up, _down, *refs):
    own, away = refs[:4], refs[4:8]
    t_ref = refs[8]
    xlo, y, core, z, xhi = coords()
    same = core == xhi
    dims = (((1,), (1,)), ((), ()))
    for n in range(N // W):
        cols = slice(n * W, (n + 1) * W)
        b, s = brow[:, cols], sj[:, cols]
        coeff = cx[cols, :]
        for src, at in ((xa, 0), (x4, EARLY)):
            rows = slice(at, at + (EARLY if at == 0 else BL))
            pull = lax.dot_general(src[: rows.stop - at, :], coeff, dims, preferred_element_type=F32)
            t_ref[rows, cols] = b * (pull - (yp[rows, cols].astype(F32) * b) * s)
    for k in range(NY):
        here, there = [], []
        for other in range(2):
            g = (xlo + other) % 2 * 4 + (y + k) % 4
            at = position((g - z + NZ) % NZ) * BL
            p, q = halves(t_ref[pl.ds(pl.multiple_of(at, BL), BL), :])
            here.append(jnp.where(same, p, q))
            there.append(jnp.where(same, q, p))
        own[k][...] = jnp.concatenate(here, axis=0)
        away[k][...] = jnp.concatenate(there, axis=0).astype(BF16)


def call(kernel, out_shape, flops, args, scratch=(), smem=(), unread=(), limit=32 * MIB):
    vm = pl.BlockSpec(memory_space=pltpu.VMEM)
    specs = [vm] * len(args)
    for i in smem:
        specs[i] = pl.BlockSpec(memory_space=pltpu.SMEM)
    for i in unread:
        specs[i] = pl.BlockSpec(memory_space=pl.ANY)
    moved = sum(x.size * x.dtype.itemsize for x in list(args) + list(out_shape))
    return pl.pallas_call(
        kernel,
        out_shape=out_shape,
        in_specs=specs,
        out_specs=[vm] * len(out_shape),
        scratch_shapes=list(scratch),
        compiler_params=pltpu.CompilerParams(vmem_limit_bytes=limit),
        cost_estimate=pl.CostEstimate(flops=flops, bytes_accessed=moved, transcendentals=0),
    )(*args)


def sds(shape, dtype):
    return jax.ShapeDtypeStruct(shape, dtype)


def wide(v):
    return v.astype(F32)


def run_text(mine, others):
    return call(
        text_kernel,
        [sds((ROWS, N), BF16), sds((N, ROWS), BF16), sds((1, N), F32), sds((N, 128), F32)],
        N * N * 64,
        list(mine) + list(others),
    )


def run_early(blocks, ypt):
    return call(
        early_kernel,
        [sds((WIDE, N), BF16), sds((N, N), F32), sds((1, N), F32)],
        2 * N * N * WIDE,
        list(blocks) + [ypt],
    )


def run_middle(left, right, part, square, pairs, log_scale, bias, yp, ypt, bcol):
    row = sds((1, N), F32)
    return call(
        middle_kernel,
        [sds((BL, N), BF16), sds((N, N), BF16), sds((N, N), BF16), row, row, row, row]
        + [sds((BL, HALF), BF16)] * 2,
        2 * N * N * ROWS,
        [left, right, part, square, pairs.reshape(1, N), log_scale, bias, yp, ypt, bcol],
        [
            pltpu.VMEM((ROWS - TAIL, N), BF16),
            pltpu.VMEM((N, LANES), F32),
            pltpu.VMEM((N, 128), F32),
        ],
        smem=(5, 6),
    )


def run_images(xa, yp, cy, arow, si):
    return call(
        image_kernel, [sds((BL, N), F32)] * 7, 2 * N * N * EARLY, [xa, yp, cy, arow, si]
    )


def run_captions(xa, x4, cx, yp, brow, sj, up, down):
    return call(
        caption_kernel,
        [sds((BL, N), F32)] * NY + [sds((BL, N), BF16)] * NY,
        2 * N * N * ROWS,
        [xa, x4, cx, yp, brow, sj, up, down],
        [pltpu.VMEM((ROWS, N), F32)],
        unread=(6, 7),
    )


def add_after(groups, earlier, dtype=F32):
    args = [v for group in groups for v in group]

    def kernel(*refs):
        outs = refs[len(args) + len(earlier) :]
        at = 0
        for out, group in zip(outs, groups):
            total = refs[at][...].astype(F32)
            for ref in refs[at + 1 : at + len(group)]:
                total = total + ref[...].astype(F32)
            out[...] = total.astype(dtype)
            at += len(group)

    return call(
        kernel,
        [sds(group[0].shape, dtype) for group in groups],
        1,
        args + list(earlier),
        unread=range(len(args), len(args) + len(earlier)),
        limit=16 * MIB,
    )


def together(*values):
    return lax.optimization_barrier(values)


def split(v):
    high = lax.reduce_precision(v, 8, 7)
    return high, lax.reduce_precision(v - high, 8, 7)


def shards(images, texts, pairs, log_scale, bias):
    other_img, other_txt = together(swap_xhi(images), swap_xlo(texts))
    up = down = jnp.concatenate([images, other_img], axis=0)
    block = jnp.concatenate([texts, other_txt], axis=0)
    ring = [[] for _ in range(NZ)]
    ring[0] = [up]
    up, down = shift_z(up, 1), shift_z(down, -1)
    behind, ahead = shift_y(block, 1), shift_y(block, -1)
    up, down, block2 = together(up, down, swap_core(block))
    ring[NZ - 1], ring[1] = [up], [down]
    up, down = shift_z(up, 1), shift_z(down, -1)
    across = shift_y(behind, 1)
    up, down, ahead2, behind2 = together(up, down, swap_core(ahead), swap_core(behind))
    ring[NZ - 2], ring[2] = [up], [down]
    up, down = shift_z(up, 1), shift_z(down, -1)
    up, down, across2 = together(up, down, swap_core(across))
    ring[NZ - 3], ring[3] = [up], [down]
    left, right = shift_z(up[:, :HALF], 1), shift_z(down[:, HALF:], -1)
    yp, ypt, brow, bcol = run_text(
        [block, ahead, across, behind], [block2, ahead2, across2, behind2]
    )
    xa, products, square = run_early([ring[k][0] for k in ORDER[:7]], ypt)

    x4, cy, cx, sj, si, arow, loss, up, down = run_middle(
        left, right, products, square, pairs, log_scale, bias, yp, ypt, bcol
    )
    up, down = shift_z(up, 1), shift_z(down, -1)
    found = run_images(xa, yp, cy, arow, si)
    terms = {k: found[i] for i, k in enumerate(ORDER[:7])}
    up = (terms[3] + jnp.pad(wide(up), ((0, 0), (0, HALF)))).astype(BF16)
    down = (terms[5] + jnp.pad(wide(down), ((0, 0), (HALF, 0)))).astype(BF16)
    (loss,) = add_after([[loss]], (up, down))
    lost = xor_z(loss, 1)
    cap = run_captions(xa, x4, cx, yp, brow, sj, up, down)
    up, down = shift_z(up, 1), shift_z(down, -1)
    got = [swap_core(cap[NY + k]) for k in range(NY)]
    up, down, lost = together(up, down, lost)
    up = (terms[2] + wide(up)).astype(BF16)
    down = (terms[6] + wide(down)).astype(BF16)
    (loss,) = add_after([[loss, lost]], (up, down))
    lost = xor_z(loss, 2)
    tup, tdown = add_after([[cap[2], got[2]], [cap[3], got[3]]], (up, down), BF16)
    tup, tdown = shift_y(tup, 1), shift_y(tdown, -1)
    up, down = shift_z(up, 1), shift_z(down, -1)
    up, down, lost = together(up, down, lost)
    up = (terms[1] + wide(up)).astype(BF16)
    down = (terms[7] + wide(down)).astype(BF16)
    (loss,) = add_after([[loss, lost]], (up, down))
    lost = xor_z(loss, 4)
    (tup,) = add_after([[cap[1], got[1], tup]], (up, down), BF16)
    tup = shift_y(tup, 1)
    up, down = shift_z(up, 1), shift_z(down, -1)
    total = terms[0] + wide(up) + wide(down)
    loss = loss + lost

    high, low = split(loss)
    rows = jnp.concatenate([high, low, jnp.zeros((6, N), F32)], axis=0)
    away = wide(swap_xhi(jnp.concatenate([total[SH:], rows], axis=0).astype(BF16)))
    image_grad = total[:SH] + away[:SH]
    loss = (high + low) + (away[SH : SH + 1] + away[SH + 1 : SH + 2])
    total = cap[0] + wide(got[0]) + wide(tup) + wide(tdown)
    text_grad = total[:SH] + wide(swap_xlo(total[SH:].astype(BF16)))
    return (loss.reshape(N), image_grad, text_grad)


def solution(mesh):
    return jax.shard_map(
        shards,
        mesh=mesh,
        in_specs=(P("col", "row"), P("row", "col"), P("row"), P(), P()),
        out_specs=(P("row"), P("col", "row"), P("row", "col")),
        check_vma=False,
    )
```

```python
import functools

import jax
import jax.numpy as jnp
from jax import lax
from jax.experimental import pallas as pl
from jax.experimental.pallas import tpu as pltpu
from jax.sharding import PartitionSpec as P

EPS = 1e-06
F32 = jnp.float32
BF16 = jnp.bfloat16
NZ, NY = 8, 4
SH = 72
BL = 2 * SH
N = 1024
HALF = N // 2
ROWS = 16 * SH
MIB = 1024 * 1024


def row_pairs(f):
    out = []
    for r in range(16):
        a, b, c = f(r // 8, (r // 2) % 4, r % 2)
        out.append((r, (a * 4 + b) * 2 + c))
    return out


def col_pairs(f):
    out = []
    for r in range(16):
        a, b = f(r // 2, r % 2)
        out.append((r, a * 2 + b))
    return out


def shift_z(v, d):
    return lax.ppermute(v, "col", col_pairs(lambda z, h: ((z + d) % NZ, h)))


def shift_y(v, d):
    return lax.ppermute(v, "row", row_pairs(lambda x, y, c: (x, (y + d) % NY, c)))


def swap_xhi(v):
    return lax.ppermute(v, "col", col_pairs(lambda z, h: (z, 1 - h)))


def swap_xlo(v):
    return lax.ppermute(v, "row", row_pairs(lambda x, y, c: (1 - x, y, c)))


def swap_core(v):
    return lax.ppermute(v, "row", row_pairs(lambda x, y, c: (x, y, 1 - c)))


def xor_z(v, b):
    return lax.ppermute(v, "col", col_pairs(lambda z, h: (z ^ b, h)))


def coords():
    row, col = lax.axis_index("row"), lax.axis_index("col")
    return row // 8, (row // 2) % 4, row % 2, col // 2, col % 2


def halves(v):
    return v[:SH], v[SH:]


def position(k):
    place = 0
    for i, block in enumerate(ORDER):
        place = jnp.where(k == block, i, place)
    return place


ORDER = (0, 1, 2, 6, 7, 3, 5, 4)
EARLY = 7 * BL
WIDE = 1024
TAIL = 896


def text_kernel(*refs):
    mine, others = refs[:4], refs[4:8]
    yp, ypt, brow, bcol = refs[8:]
    xlo, y, core, z, xhi = coords()
    same = core == xhi
    total = jnp.zeros((1, N), F32)
    for k in range(NY):
        here = halves(mine[k][...].astype(F32))
        away = halves(others[k][...].astype(F32))
        for other in range(2):
            a, b = here[other], away[other]
            block = jnp.concatenate([jnp.where(same, a, b), jnp.where(same, b, a)], axis=0)
            g = (xlo + other) % 2 * 4 + (y + k) % 4
            at = position((g - z + NZ) % NZ) * BL
            yp[pl.ds(pl.multiple_of(at, BL), BL), :] = block.astype(BF16)
            total += jnp.sum(block * block, axis=0, keepdims=True)
    brow[...] = lax.rsqrt(total + EPS)
    for c in range(N // 128):
        v = yp[:, c * 128 : (c + 1) * 128].T
        ypt[c * 128 : (c + 1) * 128, :] = v
        w = v.astype(F32)
        s = jnp.sum(w * w, axis=1, keepdims=True)
        bcol[c * 128 : (c + 1) * 128, :] = jnp.broadcast_to(lax.rsqrt(s + EPS), (128, 128))


W = 256


def early_kernel(*refs):
    blocks, ypt = refs[:7], refs[7]
    xa, part, square = refs[8:]
    total = jnp.zeros((1, N), F32)
    for i, block in enumerate(blocks):
        v = block[...]
        xa[i * BL : (i + 1) * BL, :] = v
        v = v.astype(F32)
        total += jnp.sum(v * v, axis=0, keepdims=True)
    xa[EARLY:, :] = jnp.zeros((WIDE - EARLY, N), BF16)
    square[...] = total
    for n in range(N // W):
        cols = slice(n * W, (n + 1) * W)
        part[:, cols] = jnp.dot(ypt[:, :WIDE], xa[:, cols], preferred_element_type=F32)


LANES = 512
TILE = 64
MSG = BL + 16


def encode(v):
    high = v.astype(BF16).astype(F32)
    low = v - high
    row = lax.broadcasted_iota(jnp.int32, (16, HALF), 0)
    out = jnp.zeros((16, HALF), F32)
    for i, part in enumerate((high[:, :HALF], high[:, HALF:], low[:, :HALF], low[:, HALF:])):
        out = jnp.where(row == i, part, out)
    return out.astype(BF16)


def decode(rows):
    v = rows.astype(F32)
    return jnp.concatenate([v[0:1] + v[2:3], v[1:2] + v[3:4]], axis=1)


def from_side(up, down, parity):
    z = lax.axis_index("col") // 2
    return decode(jnp.where(z % 2 == parity, up[BL:, :HALF].astype(F32), down[BL:, :HALF].astype(F32)))


def first_step_kernel(t_up, t_down, r_up, r_down, loss, m_up, m_down, pair):
    m_up[:BL, :HALF] = (t_up[:, :HALF] + r_up[:BL, :].astype(F32)).astype(BF16)
    m_up[:BL, HALF:] = t_up[:, HALF:].astype(BF16)
    m_down[:BL, :HALF] = t_down[:, :HALF].astype(BF16)
    m_down[:BL, HALF:] = (t_down[:, HALF:] + r_down[:BL, :].astype(F32)).astype(BF16)
    ride = encode(decode(encode(loss[...])) + from_side(r_up, r_down, 1))
    pair[...] = decode(ride)
    for m in (m_up, m_down):
        m[BL:, :HALF] = ride
        m[BL:, HALF:] = jnp.zeros((MSG - BL, HALF), BF16)


def step_kernel(parity, t_up, t_down, r_up, r_down, m_up, m_down, side):
    for t, r, m in ((t_up, r_up, m_up), (t_down, r_down, m_down)):
        m[:BL, :] = (t[...] + r[:BL, :].astype(F32)).astype(BF16)
        m[BL:, :] = r[BL:, :]
    side[...] = from_side(r_up, r_down, parity)


def last_step_kernel(term, r_up, r_down, pair, side1, side2, own, far, loss):
    total = term[...] + r_up[:BL, :].astype(F32) + r_down[:BL, :].astype(F32)
    own[...] = total[:SH]
    far[...] = total[SH:].astype(BF16)
    loss[...] = (pair[...] + from_side(r_up, r_down, 0)) + (side1[...] + side2[...])


def middle_kernel(
    left, right, part, square, pairs, logscale, bias, yp, ypt, bcol,
    x4, cy, cx, sj, si, arow, loss, out_left, out_right, xb, t_ref, acc_sj,
):
    x4[:, :HALF] = left[...]
    x4[:, HALF:] = right[...]
    xb[: EARLY - TAIL, :] = jnp.zeros((EARLY - TAIL, N), BF16)
    xb[EARLY - TAIL :, :] = x4[...]
    v = x4[...].astype(F32)
    a = lax.rsqrt(square[...] + jnp.sum(v * v, axis=0, keepdims=True) + EPS)
    arow[...] = a
    scale = jnp.exp(jnp.full((1, N), logscale[0], F32))
    ascale = a * scale
    shift = bias[0]
    acc_sj[...] = jnp.zeros_like(acc_sj)
    first = lax.axis_index("col") * N
    sub = TILE // 8
    strips = LANES // 128
    for n in range(N // LANES):
        cols = slice(n * LANES, (n + 1) * LANES)
        t_ref[...] = jnp.dot(ypt[:, TAIL:], xb[:, cols], preferred_element_type=F32)
        ai, asc, sc, pair = a[:, cols], ascale[:, cols], scale[:, cols], pairs[:, cols] - first

        def body(j, carry, cols=cols, ai=ai, asc=asc, sc=sc, pair=pair):
            al, asi = carry
            rows = pl.ds(pl.multiple_of(j * TILE, TILE), TILE)
            b = jnp.concatenate([bcol[rows, :]] * strips, axis=1)
            cos = ((t_ref[rows, :] + part[rows, cols]) * b) * ai
            logit = cos * sc + shift
            hit = lax.broadcasted_iota(jnp.int32, (TILE, LANES), 0) == pair - j * TILE
            e = jnp.exp(logit)
            sig = e * pltpu.reciprocal(1.0 + e)
            d = jnp.where(hit, sig - 1.0, sig)
            dc = d * cos
            cy[rows, cols] = ((d * b) * sc).astype(BF16)
            cx[rows, cols] = (d * asc).astype(BF16)
            strip = dc[:, :128]
            for m in range(1, strips):
                strip = strip + dc[:, m * 128 : (m + 1) * 128]
            acc_sj[rows, :] += strip
            e8 = e.reshape(sub, 8, LANES)
            q = e8[0]
            for m in range(1, sub):
                q = q + (e8[m] + q * e8[m])
            soft = jnp.where(q < 1e-4, (1.0 - 0.5 * q) * q, jnp.log(1.0 + q))
            al = al + soft - jnp.sum(jnp.where(hit, logit, 0.0).reshape(sub, 8, LANES), axis=0)
            asi = asi + jnp.sum(dc.reshape(sub, 8, LANES), axis=0)
            return al, asi

        zero = jnp.zeros((8, LANES), F32)
        al, asi = lax.fori_loop(0, N // TILE, body, (zero, zero))
        loss[:, cols] = jnp.sum(al, axis=0, keepdims=True)
        inner = jnp.sum(asi, axis=0, keepdims=True) * sc
        si[:, cols] = inner
        pull = jnp.dot(yp[EARLY:, :], cy[:, cols], preferred_element_type=F32)
        term = ai * (pull - (x4[:, cols].astype(F32) * ai) * inner)
        out = out_left if n * LANES < HALF else out_right
        at = n * LANES % HALF
        out[:BL, at : at + LANES] = term.astype(BF16)
    ride = encode(loss[...])
    out_left[BL:, :] = ride
    out_right[BL:, :] = ride
    sj[...] = jnp.sum(acc_sj[...].T, axis=0, keepdims=True) * scale


def image_kernel(places, xa, yp, cy, arow, si, *refs):
    outs = refs[-len(places) :]
    low, high = places[0] * BL, (places[-1] + 1) * BL
    for n in range(N // W):
        cols = slice(n * W, (n + 1) * W)
        pull = jnp.dot(yp[low:high, :], cy[:, cols], preferred_element_type=F32)
        a, s = arow[:, cols], si[:, cols]
        for i, out in zip(places, outs):
            u = xa[i * BL : (i + 1) * BL, cols].astype(F32) * a
            out[:, cols] = a * (pull[i * BL - low : (i + 1) * BL - low] - u * s)


def caption_kernel(xa, x4, cx, yp, brow, sj, _up, _down, *refs):
    own, away = refs[:4], refs[4:8]
    t_ref = refs[8]
    xlo, y, core, z, xhi = coords()
    same = core == xhi
    dims = (((1,), (1,)), ((), ()))
    for n in range(N // W):
        cols = slice(n * W, (n + 1) * W)
        b, s = brow[:, cols], sj[:, cols]
        coeff = cx[cols, :]
        for src, at in ((xa, 0), (x4, EARLY)):
            rows = slice(at, at + (EARLY if at == 0 else BL))
            pull = lax.dot_general(src[: rows.stop - at, :], coeff, dims, preferred_element_type=F32)
            t_ref[rows, cols] = b * (pull - (yp[rows, cols].astype(F32) * b) * s)
    for k in range(NY):
        here, there = [], []
        for other in range(2):
            g = (xlo + other) % 2 * 4 + (y + k) % 4
            at = position((g - z + NZ) % NZ) * BL
            p, q = halves(t_ref[pl.ds(pl.multiple_of(at, BL), BL), :])
            here.append(jnp.where(same, p, q))
            there.append(jnp.where(same, q, p))
        own[k][...] = jnp.concatenate(here, axis=0)
        away[k][...] = jnp.concatenate(there, axis=0).astype(BF16)


def call(kernel, out_shape, flops, args, scratch=(), smem=(), unread=(), limit=32 * MIB, moved=None):
    vm = pl.BlockSpec(memory_space=pltpu.VMEM)
    specs = [vm] * len(args)
    for i in smem:
        specs[i] = pl.BlockSpec(memory_space=pltpu.SMEM)
    for i in unread:
        specs[i] = pl.BlockSpec(memory_space=pl.ANY)
    if moved is None:
        moved = sum(x.size * x.dtype.itemsize for x in list(args) + list(out_shape))
    return pl.pallas_call(
        kernel,
        out_shape=out_shape,
        in_specs=specs,
        out_specs=[vm] * len(out_shape),
        scratch_shapes=list(scratch),
        compiler_params=pltpu.CompilerParams(vmem_limit_bytes=limit),
        cost_estimate=pl.CostEstimate(flops=flops, bytes_accessed=moved, transcendentals=0),
    )(*args)


def sds(shape, dtype):
    return jax.ShapeDtypeStruct(shape, dtype)


def wide(v):
    return v.astype(F32)


def run_text(mine, others):
    return call(
        text_kernel,
        [sds((ROWS, N), BF16), sds((N, ROWS), BF16), sds((1, N), F32), sds((N, 128), F32)],
        N * N * 64,
        list(mine) + list(others),
    )


def run_early(blocks, ypt):
    return call(
        early_kernel,
        [sds((WIDE, N), BF16), sds((N, N), F32), sds((1, N), F32)],
        2 * N * N * WIDE,
        list(blocks) + [ypt],
    )


def run_middle(left, right, part, square, pairs, log_scale, bias, yp, ypt, bcol):
    row = sds((1, N), F32)
    return call(
        middle_kernel,
        [sds((BL, N), BF16), sds((N, N), BF16), sds((N, N), BF16), row, row, row, row]
        + [sds((MSG, HALF), BF16)] * 2,
        2 * N * N * ROWS,
        [left, right, part, square, pairs.reshape(1, N), log_scale, bias, yp, ypt, bcol],
        [
            pltpu.VMEM((ROWS - TAIL, N), BF16),
            pltpu.VMEM((N, LANES), F32),
            pltpu.VMEM((N, 128), F32),
        ],
        smem=(5, 6),
    )


def run_images(places, xa, yp, cy, arow, si, earlier=()):
    found = call(
        functools.partial(image_kernel, places),
        [sds((BL, N), F32)] * len(places),
        2 * N * N * BL * len(places),
        [xa, yp, cy, arow, si, *earlier],
        unread=range(5, 5 + len(earlier)),
    )
    return {ORDER[i]: v for i, v in zip(places, found)}


def run_captions(xa, x4, cx, yp, brow, sj, up, down):
    return call(
        caption_kernel,
        [sds((BL, N), F32)] * NY + [sds((BL, N), BF16)] * NY,
        2 * N * N * ROWS,
        [xa, x4, cx, yp, brow, sj, up, down],
        [pltpu.VMEM((ROWS, N), F32)],
        unread=(6, 7),
    )


def add_after(groups, earlier, dtype=F32, weight=1):
    args = [v for group in groups for v in group]

    def kernel(*refs):
        outs = refs[len(args) + len(earlier) :]
        at = 0
        for out, group in zip(outs, groups):
            total = refs[at][...].astype(F32)
            for ref in refs[at + 1 : at + len(group)]:
                total = total + ref[...].astype(F32)
            out[...] = total.astype(dtype)
            at += len(group)

    return call(
        kernel,
        [sds(group[0].shape, dtype) for group in groups],
        1,
        args + list(earlier),
        unread=range(len(args), len(args) + len(earlier)),
        limit=16 * MIB,
        moved=weight,
    )


def together(*values):
    return lax.optimization_barrier(values)


def shards(images, texts, pairs, log_scale, bias):
    other_img, other_txt = swap_xhi(images), swap_xlo(texts)
    up = down = jnp.concatenate([images, other_img], axis=0)
    block = jnp.concatenate([texts, other_txt], axis=0)
    ring = [[] for _ in range(NZ)]
    ring[0] = [up]
    behind, ahead = shift_y(block, 1), shift_y(block, -1)
    across = shift_y(behind, 1)
    up, down = shift_z(up, 1), shift_z(down, -1)
    ring[NZ - 1], ring[1] = [up], [down]
    up, down = shift_z(up, 1), shift_z(down, -1)
    up, down, block2 = together(up, down, swap_core(block))
    ring[NZ - 2], ring[2] = [up], [down]
    up, down = shift_z(up, 1), shift_z(down, -1)
    ring[NZ - 3], ring[3] = [up], [down]
    left, right = shift_z(up[:, :HALF], 1), shift_z(down[:, HALF:], -1)
    yp, ypt, brow, bcol = run_text(
        [block, ahead, across, behind],
        [block2, swap_core(ahead), swap_core(across), swap_core(behind)],
    )
    xa, products, square = run_early([ring[k][0] for k in ORDER[:7]], ypt)

    x4, cy, cx, sj, si, arow, loss, up, down = run_middle(
        left, right, products, square, pairs, log_scale, bias, yp, ypt, bcol
    )
    up, down = shift_z(up, 1), shift_z(down, -1)
    terms = run_images((5, 6), xa, yp, cy, arow, si)
    message, row, half = sds((MSG, N), BF16), sds((1, N), F32), sds((SH, N), F32)
    up, down, pair = call(
        first_step_kernel, [message, message, row], 1, [terms[3], terms[5], up, down, loss]
    )
    cap = run_captions(xa, x4, cx, yp, brow, sj, up, down)
    terms |= run_images((0, 1, 2, 3, 4), xa, yp, cy, arow, si, (up, down))
    up, down = shift_z(up, 1), shift_z(down, -1)
    got = [swap_core(cap[NY + k]) for k in range(NY)]
    up, down, side1 = call(
        functools.partial(step_kernel, 0), [message, message, row], 1, [terms[2], terms[6], up, down]
    )
    sends = add_after([[cap[k], got[k]] for k in (1, 2, 3)], (up, down), BF16)
    up, down = shift_z(up, 1), shift_z(down, -1)
    found = [shift_y(v, k) for k, v in zip((1, 2, -1), sends)]
    up, down, side2 = call(
        functools.partial(step_kernel, 1), [message, message, row], 1, [terms[1], terms[7], up, down]
    )
    up, down = shift_z(up, 1), shift_z(down, -1)
    own, far, loss = call(
        last_step_kernel,
        [half, sds((SH, N), BF16), row],
        1,
        [terms[0], up, down, pair, side1, side2],
    )
    image_grad = own + wide(swap_xhi(far))
    (total,) = add_after([[cap[0], got[0], *found]], ())
    text_grad = total[:SH] + wide(swap_xlo(total[SH:].astype(BF16)))
    loss = loss + swap_xhi(loss)
    return (loss.reshape(N), image_grad, text_grad)


def solution(mesh):
    return jax.shard_map(
        shards,
        mesh=mesh,
        in_specs=(P("col", "row"), P("row", "col"), P("row"), P(), P()),
        out_specs=(P("row"), P("col", "row"), P("row", "col")),
        check_vma=False,
    )
```

```python
import functools

import jax
import jax.numpy as jnp
from jax import lax
from jax.experimental import pallas as pl
from jax.experimental.pallas import tpu as pltpu
from jax.sharding import PartitionSpec as P

EPS = 1e-06
F32 = jnp.float32
BF16 = jnp.bfloat16
NZ, NY = 8, 4
SH = 72
BL = 2 * SH
N = 1024
HALF = N // 2
ROWS = 16 * SH
MIB = 1024 * 1024


def row_pairs(f):
    out = []
    for r in range(16):
        a, b, c = f(r // 8, (r // 2) % 4, r % 2)
        out.append((r, (a * 4 + b) * 2 + c))
    return out


def col_pairs(f):
    out = []
    for r in range(16):
        a, b = f(r // 2, r % 2)
        out.append((r, a * 2 + b))
    return out


def shift_z(v, d):
    return lax.ppermute(v, "col", col_pairs(lambda z, h: ((z + d) % NZ, h)))


def shift_y(v, d):
    return lax.ppermute(v, "row", row_pairs(lambda x, y, c: (x, (y + d) % NY, c)))


def swap_xhi(v):
    return lax.ppermute(v, "col", col_pairs(lambda z, h: (z, 1 - h)))


def swap_xlo(v):
    return lax.ppermute(v, "row", row_pairs(lambda x, y, c: (1 - x, y, c)))


def swap_core(v):
    return lax.ppermute(v, "row", row_pairs(lambda x, y, c: (x, y, 1 - c)))


def xor_z(v, b):
    return lax.ppermute(v, "col", col_pairs(lambda z, h: (z ^ b, h)))


def coords():
    row, col = lax.axis_index("row"), lax.axis_index("col")
    return row // 8, (row // 2) % 4, row % 2, col // 2, col % 2


def halves(v):
    return v[:SH], v[SH:]


def position(k):
    place = 0
    for i, block in enumerate(ORDER):
        place = jnp.where(k == block, i, place)
    return place


ORDER = (0, 1, 2, 6, 7, 3, 5, 4)
EARLY = 7 * BL
WIDE = 1024
TAIL = 896


def text_kernel(*refs):
    mine, others = refs[:4], refs[4:8]
    yp, ypt, brow, bcol = refs[8:]
    xlo, y, core, z, xhi = coords()
    same = core == xhi
    total = jnp.zeros((1, N), F32)
    for k in range(NY):
        here = halves(mine[k][...].astype(F32))
        away = halves(others[k][...].astype(F32))
        for other in range(2):
            a, b = here[other], away[other]
            block = jnp.concatenate([jnp.where(same, a, b), jnp.where(same, b, a)], axis=0)
            g = (xlo + other) % 2 * 4 + (y + k) % 4
            at = position((g - z + NZ) % NZ) * BL
            yp[pl.ds(pl.multiple_of(at, BL), BL), :] = block.astype(BF16)
            total += jnp.sum(block * block, axis=0, keepdims=True)
    brow[...] = lax.rsqrt(total + EPS)
    for c in range(N // 128):
        v = yp[:, c * 128 : (c + 1) * 128].T
        ypt[c * 128 : (c + 1) * 128, :] = v
        w = v.astype(F32)
        s = jnp.sum(w * w, axis=1, keepdims=True)
        bcol[c * 128 : (c + 1) * 128, :] = jnp.broadcast_to(lax.rsqrt(s + EPS), (128, 128))


W = 256


def early_kernel(*refs):
    blocks, ypt = refs[:7], refs[7]
    xa, part, square = refs[8:]
    total = jnp.zeros((1, N), F32)
    for i, block in enumerate(blocks):
        v = block[...]
        xa[i * BL : (i + 1) * BL, :] = v
        v = v.astype(F32)
        total += jnp.sum(v * v, axis=0, keepdims=True)
    xa[EARLY:, :] = jnp.zeros((WIDE - EARLY, N), BF16)
    square[...] = total
    for n in range(N // W):
        cols = slice(n * W, (n + 1) * W)
        part[:, cols] = jnp.dot(ypt[:, :WIDE], xa[:, cols], preferred_element_type=F32)


LANES = 512
TILE = 64
MSG = BL + 16


def encode(v):
    high = v.astype(BF16).astype(F32)
    low = v - high
    row = lax.broadcasted_iota(jnp.int32, (16, HALF), 0)
    out = jnp.zeros((16, HALF), F32)
    for i, part in enumerate((high[:, :HALF], high[:, HALF:], low[:, :HALF], low[:, HALF:])):
        out = jnp.where(row == i, part, out)
    return out.astype(BF16)


def decode(rows):
    v = rows.astype(F32)
    return jnp.concatenate([v[0:1] + v[2:3], v[1:2] + v[3:4]], axis=1)


def from_side(up, down, parity):
    z = lax.axis_index("col") // 2
    return decode(jnp.where(z % 2 == parity, up[BL:, :HALF].astype(F32), down[BL:, :HALF].astype(F32)))


def first_step_kernel(t_up, t_down, r_up, r_down, loss, _cap, m_up, m_down, pair):
    m_up[:BL, :HALF] = (t_up[:, :HALF] + r_up[:BL, :].astype(F32)).astype(BF16)
    m_up[:BL, HALF:] = t_up[:, HALF:].astype(BF16)
    m_down[:BL, :HALF] = t_down[:, :HALF].astype(BF16)
    m_down[:BL, HALF:] = (t_down[:, HALF:] + r_down[:BL, :].astype(F32)).astype(BF16)
    ride = encode(decode(encode(loss[...])) + from_side(r_up, r_down, 1))
    pair[...] = decode(ride)
    for m in (m_up, m_down):
        m[BL:, :HALF] = ride
        m[BL:, HALF:] = jnp.zeros((MSG - BL, HALF), BF16)


def step_kernel(parity, t_up, t_down, r_up, r_down, m_up, m_down, side):
    for t, r, m in ((t_up, r_up, m_up), (t_down, r_down, m_down)):
        m[:BL, :] = (t[...] + r[:BL, :].astype(F32)).astype(BF16)
        m[BL:, :] = r[BL:, :]
    side[...] = from_side(r_up, r_down, parity)


def last_step_kernel(term, r_up, r_down, pair, side1, side2, own, far, loss):
    total = term[...] + r_up[:BL, :].astype(F32) + r_down[:BL, :].astype(F32)
    own[...] = total[:SH]
    far[...] = total[SH:].astype(BF16)
    loss[...] = (pair[...] + from_side(r_up, r_down, 0)) + (side1[...] + side2[...])


def middle_kernel(
    left, right, part, square, pairs, logscale, bias, yp, ypt, bcol,
    x4, cy, cx, sj, si, arow, loss, out_left, out_right, xb, t_ref, acc_sj,
):
    x4[:, :HALF] = left[...]
    x4[:, HALF:] = right[...]
    xb[: EARLY - TAIL, :] = jnp.zeros((EARLY - TAIL, N), BF16)
    xb[EARLY - TAIL :, :] = x4[...]
    v = x4[...].astype(F32)
    a = lax.rsqrt(square[...] + jnp.sum(v * v, axis=0, keepdims=True) + EPS)
    arow[...] = a
    scale = jnp.exp(jnp.full((1, N), logscale[0], F32))
    ascale = a * scale
    shift = bias[0]
    acc_sj[...] = jnp.zeros_like(acc_sj)
    first = lax.axis_index("col") * N
    sub = TILE // 8
    strips = LANES // 128
    for n in range(N // LANES):
        cols = slice(n * LANES, (n + 1) * LANES)
        t_ref[...] = jnp.dot(ypt[:, TAIL:], xb[:, cols], preferred_element_type=F32)
        ai, asc, sc, pair = a[:, cols], ascale[:, cols], scale[:, cols], pairs[:, cols] - first

        def body(j, carry, cols=cols, ai=ai, asc=asc, sc=sc, pair=pair):
            al, asi = carry
            rows = pl.ds(pl.multiple_of(j * TILE, TILE), TILE)
            b = jnp.concatenate([bcol[rows, :]] * strips, axis=1)
            cos = ((t_ref[rows, :] + part[rows, cols]) * b) * ai
            logit = cos * sc + shift
            hit = lax.broadcasted_iota(jnp.int32, (TILE, LANES), 0) == pair - j * TILE
            e = jnp.exp(logit)
            sig = e * pltpu.reciprocal(1.0 + e)
            d = jnp.where(hit, sig - 1.0, sig)
            dc = d * cos
            cy[rows, cols] = ((d * b) * sc).astype(BF16)
            cx[rows, cols] = (d * asc).astype(BF16)
            strip = dc[:, :128]
            for m in range(1, strips):
                strip = strip + dc[:, m * 128 : (m + 1) * 128]
            acc_sj[rows, :] += strip
            e8 = e.reshape(sub, 8, LANES)
            q = e8[0]
            for m in range(1, sub):
                q = q + (e8[m] + q * e8[m])
            soft = jnp.where(q < 1e-4, (1.0 - 0.5 * q) * q, jnp.log(1.0 + q))
            al = al + soft - jnp.sum(jnp.where(hit, logit, 0.0).reshape(sub, 8, LANES), axis=0)
            asi = asi + jnp.sum(dc.reshape(sub, 8, LANES), axis=0)
            return al, asi

        zero = jnp.zeros((8, LANES), F32)
        al, asi = lax.fori_loop(0, N // TILE, body, (zero, zero))
        loss[:, cols] = jnp.sum(al, axis=0, keepdims=True)
        inner = jnp.sum(asi, axis=0, keepdims=True) * sc
        si[:, cols] = inner
        pull = jnp.dot(yp[EARLY:, :], cy[:, cols], preferred_element_type=F32)
        term = ai * (pull - (x4[:, cols].astype(F32) * ai) * inner)
        out = out_left if n * LANES < HALF else out_right
        at = n * LANES % HALF
        out[:BL, at : at + LANES] = term.astype(BF16)
    ride = encode(loss[...])
    out_left[BL:, :] = ride
    out_right[BL:, :] = ride
    sj[...] = jnp.sum(acc_sj[...].T, axis=0, keepdims=True) * scale


def image_kernel(places, xa, yp, cy, arow, si, *refs):
    outs = refs[-len(places) :]
    low, high = places[0] * BL, (places[-1] + 1) * BL
    for n in range(N // W):
        cols = slice(n * W, (n + 1) * W)
        pull = jnp.dot(yp[low:high, :], cy[:, cols], preferred_element_type=F32)
        a, s = arow[:, cols], si[:, cols]
        for i, out in zip(places, outs):
            u = xa[i * BL : (i + 1) * BL, cols].astype(F32) * a
            out[:, cols] = a * (pull[i * BL - low : (i + 1) * BL - low] - u * s)


def caption_kernel(xa, x4, cx, yp, brow, sj, *refs):
    own, away = refs[:4], refs[4:8]
    t_ref = refs[8]
    xlo, y, core, z, xhi = coords()
    same = core == xhi
    dims = (((1,), (1,)), ((), ()))
    for n in range(N // W):
        cols = slice(n * W, (n + 1) * W)
        b, s = brow[:, cols], sj[:, cols]
        coeff = cx[cols, :]
        for src, at in ((xa, 0), (x4, EARLY)):
            rows = slice(at, at + (EARLY if at == 0 else BL))
            pull = lax.dot_general(src[: rows.stop - at, :], coeff, dims, preferred_element_type=F32)
            t_ref[rows, cols] = b * (pull - (yp[rows, cols].astype(F32) * b) * s)
    for k in range(NY):
        here, there = [], []
        for other in range(2):
            g = (xlo + other) % 2 * 4 + (y + k) % 4
            at = position((g - z + NZ) % NZ) * BL
            p, q = halves(t_ref[pl.ds(pl.multiple_of(at, BL), BL), :])
            here.append(jnp.where(same, p, q))
            there.append(jnp.where(same, q, p))
        own[k][...] = jnp.concatenate(here, axis=0)
        away[k][...] = jnp.concatenate(there, axis=0).astype(BF16)


def call(kernel, out_shape, flops, args, scratch=(), smem=(), unread=(), limit=32 * MIB, moved=None):
    vm = pl.BlockSpec(memory_space=pltpu.VMEM)
    specs = [vm] * len(args)
    for i in smem:
        specs[i] = pl.BlockSpec(memory_space=pltpu.SMEM)
    for i in unread:
        specs[i] = pl.BlockSpec(memory_space=pl.ANY)
    if moved is None:
        moved = sum(x.size * x.dtype.itemsize for x in list(args) + list(out_shape))
    return pl.pallas_call(
        kernel,
        out_shape=out_shape,
        in_specs=specs,
        out_specs=[vm] * len(out_shape),
        scratch_shapes=list(scratch),
        compiler_params=pltpu.CompilerParams(vmem_limit_bytes=limit),
        cost_estimate=pl.CostEstimate(flops=flops, bytes_accessed=moved, transcendentals=0),
    )(*args)


def sds(shape, dtype):
    return jax.ShapeDtypeStruct(shape, dtype)


def wide(v):
    return v.astype(F32)


def run_text(mine, others):
    return call(
        text_kernel,
        [sds((ROWS, N), BF16), sds((N, ROWS), BF16), sds((1, N), F32), sds((N, 128), F32)],
        N * N * 64,
        list(mine) + list(others),
    )


def run_early(blocks, ypt):
    return call(
        early_kernel,
        [sds((WIDE, N), BF16), sds((N, N), F32), sds((1, N), F32)],
        2 * N * N * WIDE,
        list(blocks) + [ypt],
    )


def run_middle(left, right, part, square, pairs, log_scale, bias, yp, ypt, bcol):
    row = sds((1, N), F32)
    return call(
        middle_kernel,
        [sds((BL, N), BF16), sds((N, N), BF16), sds((N, N), BF16), row, row, row, row]
        + [sds((MSG, HALF), BF16)] * 2,
        2 * N * N * ROWS,
        [left, right, part, square, pairs.reshape(1, N), log_scale, bias, yp, ypt, bcol],
        [
            pltpu.VMEM((ROWS - TAIL, N), BF16),
            pltpu.VMEM((N, LANES), F32),
            pltpu.VMEM((N, 128), F32),
        ],
        smem=(5, 6),
    )


def run_images(places, xa, yp, cy, arow, si, earlier=()):
    found = call(
        functools.partial(image_kernel, places),
        [sds((BL, N), F32)] * len(places),
        2 * N * N * BL * len(places),
        [xa, yp, cy, arow, si, *earlier],
        unread=range(5, 5 + len(earlier)),
    )
    return {ORDER[i]: v for i, v in zip(places, found)}


def run_captions(xa, x4, cx, yp, brow, sj):
    return call(
        caption_kernel,
        [sds((BL, N), F32)] * NY + [sds((BL, N), BF16)] * NY,
        2 * N * N * ROWS,
        [xa, x4, cx, yp, brow, sj],
        [pltpu.VMEM((ROWS, N), F32)],
    )


def add_after(groups, earlier, dtype=F32, weight=1):
    args = [v for group in groups for v in group]

    def kernel(*refs):
        outs = refs[len(args) + len(earlier) :]
        at = 0
        for out, group in zip(outs, groups):
            total = refs[at][...].astype(F32)
            for ref in refs[at + 1 : at + len(group)]:
                total = total + ref[...].astype(F32)
            out[...] = total.astype(dtype)
            at += len(group)

    return call(
        kernel,
        [sds(group[0].shape, dtype) for group in groups],
        1,
        args + list(earlier),
        unread=range(len(args), len(args) + len(earlier)),
        limit=16 * MIB,
        moved=weight,
    )


def together(*values):
    return lax.optimization_barrier(values)


def shards(images, texts, pairs, log_scale, bias):
    other_img, other_txt = swap_xhi(images), swap_xlo(texts)
    up = down = jnp.concatenate([images, other_img], axis=0)
    block = jnp.concatenate([texts, other_txt], axis=0)
    ring = [[] for _ in range(NZ)]
    ring[0] = [up]
    behind, ahead = shift_y(block, 1), shift_y(block, -1)
    across = shift_y(behind, 1)
    up, down = shift_z(up, 1), shift_z(down, -1)
    ring[NZ - 1], ring[1] = [up], [down]
    up, down = shift_z(up, 1), shift_z(down, -1)
    up, down, block2 = together(up, down, swap_core(block))
    ring[NZ - 2], ring[2] = [up], [down]
    up, down = shift_z(up, 1), shift_z(down, -1)
    ring[NZ - 3], ring[3] = [up], [down]
    left, right = shift_z(up[:, :HALF], 1), shift_z(down[:, HALF:], -1)
    yp, ypt, brow, bcol = run_text(
        [block, ahead, across, behind],
        [block2, swap_core(ahead), swap_core(across), swap_core(behind)],
    )
    xa, products, square = run_early([ring[k][0] for k in ORDER[:7]], ypt)

    x4, cy, cx, sj, si, arow, loss, up, down = run_middle(
        left, right, products, square, pairs, log_scale, bias, yp, ypt, bcol
    )
    up, down = shift_z(up, 1), shift_z(down, -1)
    terms = run_images((5, 6), xa, yp, cy, arow, si)
    cap = run_captions(xa, x4, cx, yp, brow, sj)
    message, row, half = sds((MSG, N), BF16), sds((1, N), F32), sds((SH, N), F32)
    up, down, pair = call(
        first_step_kernel,
        [message, message, row],
        1,
        [terms[3], terms[5], up, down, loss, cap[NY]],
        unread=(5,),
    )
    terms |= run_images((0, 1, 2, 3, 4), xa, yp, cy, arow, si, (up, down))
    up, down = shift_z(up, 1), shift_z(down, -1)
    got = [swap_core(cap[NY + k]) for k in range(NY)]
    up, down, side1 = call(
        functools.partial(step_kernel, 0), [message, message, row], 1, [terms[2], terms[6], up, down]
    )
    sends = add_after([[cap[k], got[k]] for k in (1, 2, 3)], (up, down), BF16)
    up, down = shift_z(up, 1), shift_z(down, -1)
    found = [shift_y(v, k) for k, v in zip((1, 2, -1), sends)]
    up, down, side2 = call(
        functools.partial(step_kernel, 1), [message, message, row], 1, [terms[1], terms[7], up, down]
    )
    up, down = shift_z(up, 1), shift_z(down, -1)
    own, far, loss = call(
        last_step_kernel,
        [half, sds((SH, N), BF16), row],
        1,
        [terms[0], up, down, pair, side1, side2],
    )
    image_grad = own + wide(swap_xhi(far))
    (total,) = add_after([[cap[0], got[0], *found]], ())
    text_grad = total[:SH] + wide(swap_xlo(total[SH:].astype(BF16)))
    loss = loss + swap_xhi(loss)
    return (loss.reshape(N), image_grad, text_grad)


def solution(mesh):
    return jax.shard_map(
        shards,
        mesh=mesh,
        in_specs=(P("col", "row"), P("row", "col"), P("row"), P(), P()),
        out_specs=(P("row"), P("col", "row"), P("row", "col")),
        check_vma=False,
    )
```

```python
import functools

import jax
import jax.numpy as jnp
from jax import lax
from jax.experimental import pallas as pl
from jax.experimental.pallas import tpu as pltpu
from jax.sharding import PartitionSpec as P

EPS = 1e-06
F32 = jnp.float32
BF16 = jnp.bfloat16
NZ, NY = 8, 4
SH = 72
BL = 2 * SH
N = 1024
HALF = N // 2
ROWS = 16 * SH
MIB = 1024 * 1024


def row_pairs(f):
    out = []
    for r in range(16):
        a, b, c = f(r // 8, (r // 2) % 4, r % 2)
        out.append((r, (a * 4 + b) * 2 + c))
    return out


def col_pairs(f):
    out = []
    for r in range(16):
        a, b = f(r // 2, r % 2)
        out.append((r, a * 2 + b))
    return out


def shift_z(v, d):
    return lax.ppermute(v, "col", col_pairs(lambda z, h: ((z + d) % NZ, h)))


def shift_y(v, d):
    return lax.ppermute(v, "row", row_pairs(lambda x, y, c: (x, (y + d) % NY, c)))


def swap_xhi(v):
    return lax.ppermute(v, "col", col_pairs(lambda z, h: (z, 1 - h)))


def swap_xlo(v):
    return lax.ppermute(v, "row", row_pairs(lambda x, y, c: (1 - x, y, c)))


def swap_core(v):
    return lax.ppermute(v, "row", row_pairs(lambda x, y, c: (x, y, 1 - c)))


def xor_z(v, b):
    return lax.ppermute(v, "col", col_pairs(lambda z, h: (z ^ b, h)))


def coords():
    row, col = lax.axis_index("row"), lax.axis_index("col")
    return row // 8, (row // 2) % 4, row % 2, col // 2, col % 2


def halves(v):
    return v[:SH], v[SH:]


def position(k):
    place = 0
    for i, block in enumerate(ORDER):
        place = jnp.where(k == block, i, place)
    return place


ORDER = (0, 1, 2, 6, 7, 3, 5, 4)
EARLY = 7 * BL
WIDE = 1024
TAIL = 896


def text_kernel(*refs):
    mine, others = refs[:4], refs[4:8]
    yp, ypt, brow, bcol = refs[8:]
    xlo, y, core, z, xhi = coords()
    same = core == xhi
    total = jnp.zeros((1, N), F32)
    for k in range(NY):
        here = halves(mine[k][...].astype(F32))
        away = halves(others[k][...].astype(F32))
        for other in range(2):
            a, b = here[other], away[other]
            block = jnp.concatenate([jnp.where(same, a, b), jnp.where(same, b, a)], axis=0)
            g = (xlo + other) % 2 * 4 + (y + k) % 4
            at = position((g - z + NZ) % NZ) * BL
            yp[pl.ds(pl.multiple_of(at, BL), BL), :] = block.astype(BF16)
            total += jnp.sum(block * block, axis=0, keepdims=True)
    brow[...] = lax.rsqrt(total + EPS)
    for c in range(N // 128):
        v = yp[:, c * 128 : (c + 1) * 128].T
        ypt[c * 128 : (c + 1) * 128, :] = v
        w = v.astype(F32)
        s = jnp.sum(w * w, axis=1, keepdims=True)
        bcol[c * 128 : (c + 1) * 128, :] = jnp.broadcast_to(lax.rsqrt(s + EPS), (128, 128))


W = 256


def early_kernel(*refs):
    blocks, ypt = refs[:7], refs[7]
    xa, part, square = refs[8:]
    total = jnp.zeros((1, N), F32)
    for i, block in enumerate(blocks):
        v = block[...]
        xa[i * BL : (i + 1) * BL, :] = v
        v = v.astype(F32)
        total += jnp.sum(v * v, axis=0, keepdims=True)
    xa[EARLY:, :] = jnp.zeros((WIDE - EARLY, N), BF16)
    square[...] = total
    for n in range(N // W):
        cols = slice(n * W, (n + 1) * W)
        part[:, cols] = jnp.dot(ypt[:, :WIDE], xa[:, cols], preferred_element_type=F32)


LANES = 512
TILE = 64
MSG = BL + 16


def encode(v):
    high = v.astype(BF16).astype(F32)
    low = v - high
    row = lax.broadcasted_iota(jnp.int32, (16, HALF), 0)
    out = jnp.zeros((16, HALF), F32)
    for i, part in enumerate((high[:, :HALF], high[:, HALF:], low[:, :HALF], low[:, HALF:])):
        out = jnp.where(row == i, part, out)
    return out.astype(BF16)


def decode(rows):
    v = rows.astype(F32)
    return jnp.concatenate([v[0:1] + v[2:3], v[1:2] + v[3:4]], axis=1)


def from_side(up, down, parity):
    z = lax.axis_index("col") // 2
    return decode(jnp.where(z % 2 == parity, up[BL:, :HALF].astype(F32), down[BL:, :HALF].astype(F32)))


def first_step_kernel(t_up, t_down, r_up, r_down, loss, _cap, m_up, m_down, pair):
    m_up[:BL, :HALF] = (t_up[:, :HALF] + r_up[:BL, :].astype(F32)).astype(BF16)
    m_up[:BL, HALF:] = t_up[:, HALF:].astype(BF16)
    m_down[:BL, :HALF] = t_down[:, :HALF].astype(BF16)
    m_down[:BL, HALF:] = (t_down[:, HALF:] + r_down[:BL, :].astype(F32)).astype(BF16)
    ride = encode(decode(encode(loss[...])) + from_side(r_up, r_down, 1))
    pair[...] = decode(ride)
    for m in (m_up, m_down):
        m[BL:, :HALF] = ride
        m[BL:, HALF:] = jnp.zeros((MSG - BL, HALF), BF16)


def step_kernel(parity, t_up, t_down, r_up, r_down, m_up, m_down, side):
    for t, r, m in ((t_up, r_up, m_up), (t_down, r_down, m_down)):
        m[:BL, :] = (t[...] + r[:BL, :].astype(F32)).astype(BF16)
        m[BL:, :] = r[BL:, :]
    side[...] = from_side(r_up, r_down, parity)


def last_step_kernel(term, r_up, r_down, pair, side1, side2, own, far, loss):
    total = term[...] + r_up[:BL, :].astype(F32) + r_down[:BL, :].astype(F32)
    own[...] = total[:SH]
    far[...] = total[SH:].astype(BF16)
    loss[...] = (pair[...] + from_side(r_up, r_down, 0)) + (side1[...] + side2[...])


def middle_kernel(
    left, right, part, square, pairs, logscale, bias, yp, ypt, bcol,
    x4, cy, cx, sj, si, arow, loss, out_left, out_right, xb, t_ref, acc_sj,
):
    x4[:, :HALF] = left[...]
    x4[:, HALF:] = right[...]
    xb[: EARLY - TAIL, :] = jnp.zeros((EARLY - TAIL, N), BF16)
    xb[EARLY - TAIL :, :] = x4[...]
    v = x4[...].astype(F32)
    a = lax.rsqrt(square[...] + jnp.sum(v * v, axis=0, keepdims=True) + EPS)
    arow[...] = a
    scale = jnp.exp(jnp.full((1, N), logscale[0], F32))
    ascale = a * scale
    shift = bias[0]
    acc_sj[...] = jnp.zeros_like(acc_sj)
    first = lax.axis_index("col") * N
    sub = TILE // 8
    strips = LANES // 128
    for n in range(N // LANES):
        cols = slice(n * LANES, (n + 1) * LANES)
        t_ref[...] = jnp.dot(ypt[:, TAIL:], xb[:, cols], preferred_element_type=F32)
        ai, asc, sc, pair = a[:, cols], ascale[:, cols], scale[:, cols], pairs[:, cols] - first

        def body(j, carry, cols=cols, ai=ai, asc=asc, sc=sc, pair=pair):
            al, asi = carry
            rows = pl.ds(pl.multiple_of(j * TILE, TILE), TILE)
            b = jnp.concatenate([bcol[rows, :]] * strips, axis=1)
            cos = ((t_ref[rows, :] + part[rows, cols]) * b) * ai
            logit = cos * sc + shift
            hit = lax.broadcasted_iota(jnp.int32, (TILE, LANES), 0) == pair - j * TILE
            e = jnp.exp(logit)
            sig = e * pltpu.reciprocal(1.0 + e)
            d = jnp.where(hit, sig - 1.0, sig)
            dc = d * cos
            cy[rows, cols] = ((d * b) * sc).astype(BF16)
            cx[rows, cols] = (d * asc).astype(BF16)
            strip = dc[:, :128]
            for m in range(1, strips):
                strip = strip + dc[:, m * 128 : (m + 1) * 128]
            acc_sj[rows, :] += strip
            e8 = e.reshape(sub, 8, LANES)
            q = e8[0]
            for m in range(1, sub):
                q = q + (e8[m] + q * e8[m])
            soft = jnp.where(q < 1e-4, (1.0 - 0.5 * q) * q, jnp.log(1.0 + q))
            al = al + soft - jnp.sum(jnp.where(hit, logit, 0.0).reshape(sub, 8, LANES), axis=0)
            asi = asi + jnp.sum(dc.reshape(sub, 8, LANES), axis=0)
            return al, asi

        zero = jnp.zeros((8, LANES), F32)
        al, asi = lax.fori_loop(0, N // TILE, body, (zero, zero))
        loss[:, cols] = jnp.sum(al, axis=0, keepdims=True)
        inner = jnp.sum(asi, axis=0, keepdims=True) * sc
        si[:, cols] = inner
        pull = jnp.dot(yp[EARLY:, :], cy[:, cols], preferred_element_type=F32)
        term = ai * (pull - (x4[:, cols].astype(F32) * ai) * inner)
        out = out_left if n * LANES < HALF else out_right
        at = n * LANES % HALF
        out[:BL, at : at + LANES] = term.astype(BF16)
    ride = encode(loss[...])
    out_left[BL:, :] = ride
    out_right[BL:, :] = ride
    sj[...] = jnp.sum(acc_sj[...].T, axis=0, keepdims=True) * scale


def image_kernel(places, xa, yp, cy, arow, si, *refs):
    outs = refs[-len(places) :]
    low, high = places[0] * BL, (places[-1] + 1) * BL
    for n in range(N // W):
        cols = slice(n * W, (n + 1) * W)
        pull = jnp.dot(yp[low:high, :], cy[:, cols], preferred_element_type=F32)
        a, s = arow[:, cols], si[:, cols]
        for i, out in zip(places, outs):
            u = xa[i * BL : (i + 1) * BL, cols].astype(F32) * a
            out[:, cols] = a * (pull[i * BL - low : (i + 1) * BL - low] - u * s)


def caption_kernel(xa, x4, cx, yp, brow, sj, *refs):
    own, away = refs[:4], refs[4:8]
    t_ref = refs[8]
    xlo, y, core, z, xhi = coords()
    same = core == xhi
    dims = (((1,), (1,)), ((), ()))
    for n in range(N // W):
        cols = slice(n * W, (n + 1) * W)
        b, s = brow[:, cols], sj[:, cols]
        coeff = cx[cols, :]
        for src, at in ((xa, 0), (x4, EARLY)):
            rows = slice(at, at + (EARLY if at == 0 else BL))
            pull = lax.dot_general(src[: rows.stop - at, :], coeff, dims, preferred_element_type=F32)
            t_ref[rows, cols] = b * (pull - (yp[rows, cols].astype(F32) * b) * s)
    for k in range(NY):
        here, there = [], []
        for other in range(2):
            g = (xlo + other) % 2 * 4 + (y + k) % 4
            at = position((g - z + NZ) % NZ) * BL
            p, q = halves(t_ref[pl.ds(pl.multiple_of(at, BL), BL), :])
            here.append(jnp.where(same, p, q))
            there.append(jnp.where(same, q, p))
        own[k][...] = jnp.concatenate(here, axis=0)
        away[k][...] = jnp.concatenate(there, axis=0).astype(BF16)


def call(kernel, out_shape, flops, args, scratch=(), smem=(), unread=(), limit=32 * MIB, moved=None):
    vm = pl.BlockSpec(memory_space=pltpu.VMEM)
    specs = [vm] * len(args)
    for i in smem:
        specs[i] = pl.BlockSpec(memory_space=pltpu.SMEM)
    for i in unread:
        specs[i] = pl.BlockSpec(memory_space=pl.ANY)
    if moved is None:
        moved = sum(x.size * x.dtype.itemsize for x in list(args) + list(out_shape))
    return pl.pallas_call(
        kernel,
        out_shape=out_shape,
        in_specs=specs,
        out_specs=[vm] * len(out_shape),
        scratch_shapes=list(scratch),
        compiler_params=pltpu.CompilerParams(vmem_limit_bytes=limit),
        cost_estimate=pl.CostEstimate(flops=flops, bytes_accessed=moved, transcendentals=0),
    )(*args)


def sds(shape, dtype):
    return jax.ShapeDtypeStruct(shape, dtype)


def wide(v):
    return v.astype(F32)


def run_text(mine, others):
    return call(
        text_kernel,
        [sds((ROWS, N), BF16), sds((N, ROWS), BF16), sds((1, N), F32), sds((N, 128), F32)],
        N * N * 64,
        list(mine) + list(others),
    )


def run_early(blocks, ypt):
    return call(
        early_kernel,
        [sds((WIDE, N), BF16), sds((N, N), F32), sds((1, N), F32)],
        2 * N * N * WIDE,
        list(blocks) + [ypt],
    )


def run_middle(left, right, part, square, pairs, log_scale, bias, yp, ypt, bcol):
    row = sds((1, N), F32)
    return call(
        middle_kernel,
        [sds((BL, N), BF16), sds((N, N), BF16), sds((N, N), BF16), row, row, row, row]
        + [sds((MSG, HALF), BF16)] * 2,
        2 * N * N * ROWS,
        [left, right, part, square, pairs.reshape(1, N), log_scale, bias, yp, ypt, bcol],
        [
            pltpu.VMEM((ROWS - TAIL, N), BF16),
            pltpu.VMEM((N, LANES), F32),
            pltpu.VMEM((N, 128), F32),
        ],
        smem=(5, 6),
    )


def run_images(places, xa, yp, cy, arow, si, earlier=()):
    found = call(
        functools.partial(image_kernel, places),
        [sds((BL, N), F32)] * len(places),
        2 * N * N * BL * len(places),
        [xa, yp, cy, arow, si, *earlier],
        unread=range(5, 5 + len(earlier)),
    )
    return {ORDER[i]: v for i, v in zip(places, found)}


def run_captions(xa, x4, cx, yp, brow, sj):
    return call(
        caption_kernel,
        [sds((BL, N), F32)] * NY + [sds((BL, N), BF16)] * NY,
        2 * N * N * ROWS,
        [xa, x4, cx, yp, brow, sj],
        [pltpu.VMEM((ROWS, N), F32)],
    )


def add_after(groups, earlier, dtype=F32, weight=1):
    args = [v for group in groups for v in group]

    def kernel(*refs):
        outs = refs[len(args) + len(earlier) :]
        at = 0
        for out, group in zip(outs, groups):
            total = refs[at][...].astype(F32)
            for ref in refs[at + 1 : at + len(group)]:
                total = total + ref[...].astype(F32)
            out[...] = total.astype(dtype)
            at += len(group)

    return call(
        kernel,
        [sds(group[0].shape, dtype) for group in groups],
        1,
        args + list(earlier),
        unread=range(len(args), len(args) + len(earlier)),
        limit=16 * MIB,
        moved=weight,
    )


def together(*values):
    return lax.optimization_barrier(values)


def shards(images, texts, pairs, log_scale, bias):
    other_img, other_txt = swap_xhi(images), swap_xlo(texts)
    up = down = jnp.concatenate([images, other_img], axis=0)
    block = jnp.concatenate([texts, other_txt], axis=0)
    ring = [[] for _ in range(NZ)]
    ring[0] = [up]
    behind, ahead = shift_y(block, 1), shift_y(block, -1)
    across = shift_y(behind, 1)
    up, down = shift_z(up, 1), shift_z(down, -1)
    ring[NZ - 1], ring[1] = [up], [down]
    up, down = shift_z(up, 1), shift_z(down, -1)
    up, down, block2 = together(up, down, swap_core(block))
    ring[NZ - 2], ring[2] = [up], [down]
    up, down = shift_z(up, 1), shift_z(down, -1)
    ring[NZ - 3], ring[3] = [up], [down]
    left, right = shift_z(up[:, :HALF], 1), shift_z(down[:, HALF:], -1)
    yp, ypt, brow, bcol = run_text(
        [block, ahead, across, behind],
        [block2, swap_core(ahead), swap_core(across), swap_core(behind)],
    )
    xa, products, square = run_early([ring[k][0] for k in ORDER[:7]], ypt)

    x4, cy, cx, sj, si, arow, loss, up, down = run_middle(
        left, right, products, square, pairs, log_scale, bias, yp, ypt, bcol
    )
    up, down = shift_z(up, 1), shift_z(down, -1)
    terms = run_images((5, 6), xa, yp, cy, arow, si)
    cap = run_captions(xa, x4, cx, yp, brow, sj)
    message, row, half = sds((MSG, N), BF16), sds((1, N), F32), sds((SH, N), F32)
    up, down, pair = call(
        first_step_kernel,
        [message, message, row],
        1,
        [terms[3], terms[5], up, down, loss, cap[NY]],
        unread=(5,),
    )
    terms |= run_images((0, 1, 2, 3, 4), xa, yp, cy, arow, si, (up, down))
    up, down = shift_z(up, 1), shift_z(down, -1)
    got = [swap_core(cap[NY + k]) for k in range(NY)]
    up, down, *got[1:4] = together(up, down, *got[1:4])
    up, down, side1 = call(
        functools.partial(step_kernel, 0), [message, message, row], 1, [terms[2], terms[6], up, down]
    )
    sends = add_after([[cap[k], got[k]] for k in (1, 2, 3)], (up, down), BF16)
    up, down = shift_z(up, 1), shift_z(down, -1)
    found = [shift_y(v, k) for k, v in zip((1, 2, -1), sends)]
    up, down, side2 = call(
        functools.partial(step_kernel, 1), [message, message, row], 1, [terms[1], terms[7], up, down]
    )
    up, down = shift_z(up, 1), shift_z(down, -1)
    own, far, loss = call(
        last_step_kernel,
        [half, sds((SH, N), BF16), row],
        1,
        [terms[0], up, down, pair, side1, side2],
    )
    image_grad = own + wide(swap_xhi(far))
    (total,) = add_after([[cap[0], got[0], *found]], ())
    text_grad = total[:SH] + wide(swap_xlo(total[SH:].astype(BF16)))
    loss = loss + swap_xhi(loss)
    return (loss.reshape(N), image_grad, text_grad)


def solution(mesh):
    return jax.shard_map(
        shards,
        mesh=mesh,
        in_specs=(P("col", "row"), P("row", "col"), P("row"), P(), P()),
        out_specs=(P("row"), P("col", "row"), P("row", "col")),
        check_vma=False,
    )
```
